256 devices in a mesh: sx: 8 (over z), sy: 8 (over y, core), batch: 4 (over x).
Axes of the slice: x: 4, y: 4, z: 8, core: 2. Of those that a mesh axis runs over, the one named last changes fastest.
Arguments:
- volume: bfloat16 [4, 64, 32, 128, 128], P('batch', None, 'sx', 'sy'), may hold values from -40 to 40
- conv_weight: bfloat16 [64, 64, 3, 3, 3], replicated, may hold values from -0.15625 to 0.15625
- out_gain: float32 [64], replicated, may hold values from 0.5 to 1.5
- out_shift: float32 [64], replicated, may hold values from -3 to 3
Outputs:
- whitened: float32 [4, 64, 32, 128, 128], P('batch', None, 'sx', 'sy')
The draws below stay inside these ranges and needn't reach their ends.
All inputs are finite; a program needn't handle non-finite values.
Results may differ from the reference program's by a relative error of at most 0.0007.
Values may be sent and summed in bfloat16 or wider, within the bound.
A program may use at most 64 MiB of HBM per device.

```python
import jax
import jax.numpy as jnp
from jax import lax

C = 64
NS_ITERS = 5
SAMPLES = 4
NX = 32
NY = 128
NZ = 128


def draw_volume(key, part):
    key_chan = jax.random.fold_in(key, 11)
    key_base = jax.random.fold_in(key, 12)
    key_coarse = jax.random.fold_in(key, 14)
    key_mask = jax.random.fold_in(key, 15)
    key_amp = jax.random.fold_in(key, 16)
    key_dir = jax.random.fold_in(key, 17)
    channel_scale = 10.0 ** jax.random.uniform(key_chan, (C,), jnp.float32)
    position = jnp.arange(NX, dtype=jnp.float32) / NX
    envelope = 3.0 ** position
    coarse = jax.random.truncated_normal(key_coarse, -3.0, 3.0, (SAMPLES, 1, NX // 4 + 1, NY // 4 + 1, NZ // 4 + 1), jnp.float32)
    modulation = jnp.exp(0.6 * coarse)
    modulation = jnp.take(modulation, jnp.arange(NX, dtype=jnp.int32) // 4, axis=2)
    modulation = jnp.take(modulation, jnp.arange(NY, dtype=jnp.int32) // 4, axis=3)
    modulation = jnp.take(modulation, jnp.arange(NZ, dtype=jnp.int32) // 4, axis=4)
    base = jax.random.truncated_normal(key_base, -4.0, 4.0, (SAMPLES, C, NX, NY, NZ), jnp.float32)
    bulk = base * channel_scale[None, :, None, None, None] * modulation * 0.02
    pair_shape = (SAMPLES, 1, NX, NY, NZ // 2)
    present = (jax.random.randint(key_mask, pair_shape, 0, 1024) == 0).astype(jnp.float32)
    amplitude = 2.0 * 3.75 ** jax.random.uniform(key_amp, pair_shape, jnp.float32)
    direction = jax.random.uniform(key_dir, (SAMPLES, C, NX, NY, NZ // 2), jnp.float32, -1.732, 1.732)
    clumps = jnp.repeat(present * amplitude * direction, 2, axis=4)
    values = (bulk + clumps) * envelope[None, None, :, None, None]
    values = jnp.clip(values, -39.5, 39.5)
    return values.astype(jnp.bfloat16)


def bell_draw(own_key, dims, spread, bound, kind=jnp.bfloat16):
    result = jax.random.normal(own_key, dims, jnp.float32) * spread
    return jnp.minimum(jnp.maximum(result, -bound), bound).astype(kind)


def setup_inputs(seed: int = 0) -> dict:
    splits = jax.random.split(jax.random.key(seed), 5)
    volume = draw_volume(jax.random.fold_in(splits[4], 71), 0)
    conv_weight = bell_draw(splits[1], (C, C, 3, 3, 3), (27 * C) ** -0.5, 0.15625)
    out_gain = jnp.clip(1.0 + 0.1 * jax.random.normal(splits[2], (C,), jnp.float32), 0.5, 1.5)
    out_shift = bell_draw(splits[3], (C,), 0.5, 3.0, jnp.float32)
    return {"volume": volume, "conv_weight": conv_weight, "out_gain": out_gain, "out_shift": out_shift}


def conv_one(sample, kernel):
    return lax.conv_general_dilated(sample[None].astype(jnp.float32), kernel.astype(jnp.float32), (1, 1, 1), [(1, 1), (1, 1), (1, 1)], dimension_numbers=('NCDHW', 'OIDHW', 'NCDHW'), precision=lax.Precision.HIGHEST)[0]

def reference(volume, conv_weight, out_gain, out_shift):
    response = lax.map(lambda sample: conv_one(sample, conv_weight), volume)
    count = SAMPLES * NX * NY * NZ
    channel_mean = lax.optimization_barrier(jnp.sum(response, axis=(0, 2, 3, 4))) / count
    centered = response - channel_mean[None, :, None, None, None]
    covariance = jnp.einsum('scxyz,sdxyz->cd', centered, centered, precision=lax.Precision.HIGHEST) / count
    sigma = covariance + 1e-05 * jnp.eye(C, dtype=jnp.float32)
    trace_total = jnp.trace(sigma)
    normed = sigma / trace_total
    factor = jnp.eye(C, dtype=jnp.float32)
    for turn in range(NS_ITERS):
        cubed = jnp.dot(jnp.dot(factor, factor, precision=lax.Precision.HIGHEST), factor, precision=lax.Precision.HIGHEST)
        factor = 1.5 * factor - 0.5 * jnp.dot(cubed, normed, precision=lax.Precision.HIGHEST)
    whiten = factor / jnp.sqrt(trace_total)
    mixed = jnp.einsum('cd,sdxyz->scxyz', whiten, centered, precision=lax.Precision.HIGHEST)
    return out_gain[None, :, None, None, None] * mixed + out_shift[None, :, None, None, None]
```

```python
import jax
import jax.numpy as jnp
from jax import lax
from jax.experimental import pallas as pl
from jax.experimental.pallas import tpu as pltpu
from jax.sharding import PartitionSpec as P

NS_ITERS = 5
C = 64
BX = 4
BY = 16
NZ = 128
LOCAL = BX * BY * NZ
MESH = pl.DeviceIdType.MESH
F32 = jnp.float32
BF16 = jnp.bfloat16
HIGHEST = lax.Precision.HIGHEST
PAIRS = ((1, 2), (0, 3))


def split(v):
    hi = v.astype(BF16)
    lo = (v - hi.astype(F32)).astype(BF16)
    return hi, lo


def nn(a, b):
    return lax.dot_general(a, b, (((1,), (0,)), ((), ())), preferred_element_type=F32)


def mm(a, b):
    ah, al = split(a)
    bh, bl = split(b)
    return nn(ah, bh) + (nn(ah, bl) + nn(al, bh))


def body(
    sizes,
    vol,
    weight,
    gain,
    shift,
    out,
    vin,
    wide,
    cells,
    win,
    toep,
    held,
    gram,
    sums,
    centre,
    moved_y,
    moved_b,
    moved_x,
    staged,
    vec,
    load_sem,
    wsem,
    vsem,
    xs_send,
    xs_recv,
    ys_send,
    ys_recv,
    cs_send,
    cs_recv,
    ry_send,
    ry_recv,
    rb_send,
    rb_recv,
    rx_send,
    rx_recv,
    out_sem,
):
    n_x, n_y, n_b = sizes
    sx = lax.axis_index("sx")
    sy = lax.axis_index("sy")
    sb = lax.axis_index("batch")

    def at(n, i, k):
        return lax.rem(i + (k + n), n)

    loads = []
    for k, x in enumerate((0, 3, 1, 2)):
        cp = pltpu.make_async_copy(vol.at[0, :, x], vin.at[x], load_sem.at[k])
        cp.start()
        loads.append(cp)
    wcp = pltpu.make_async_copy(weight, win, wsem)
    wcp.start()
    gcp = pltpu.make_async_copy(gain, vec.at[pl.ds(0, 1)], vsem.at[0])
    gcp.start()
    hcp = pltpu.make_async_copy(shift, vec.at[pl.ds(1, 1)], vsem.at[1])
    hcp.start()

    barrier = pltpu.get_barrier_semaphore()
    greeted = 0
    for k in range(1, n_x):
        pl.semaphore_signal(barrier, inc=1, device_id={"sx": at(n_x, sx, k)}, device_id_type=MESH)
        greeted += 1
    for k in range(1, n_y):
        pl.semaphore_signal(barrier, inc=1, device_id={"sy": at(n_y, sy, k)}, device_id_type=MESH)
        greeted += 1
    for k in range(1, n_b):
        pl.semaphore_signal(barrier, inc=1, device_id={"batch": at(n_b, sb, k)}, device_id_type=MESH)
        greeted += 1
    for dx in (-1, 1):
        for dy in (-1, 1):
            pl.semaphore_signal(
                barrier,
                inc=1,
                device_id={"sx": at(n_x, sx, dx), "sy": at(n_y, sy, dy)},
                device_id_type=MESH,
            )
            greeted += 1

    def relay(x):
        wide[...] = vin[x].astype(F32).reshape(C * BY, NZ)
        for y in range(BY):
            cells[x + 1, y + 1] = wide[pl.ds(y, C, stride=BY), :].astype(BF16)

    loads[0].wait()
    relay(0)
    loads[1].wait()
    relay(3)
    pl.semaphore_wait(barrier, greeted)

    sends = []

    def send(src, dst, s_sem, r_sem, dev):
        cp = pltpu.make_async_remote_copy(
            src_ref=src, dst_ref=dst, send_sem=s_sem, recv_sem=r_sem, device_id=dev, device_id_type=MESH
        )
        cp.start()
        sends.append(cp)
        return cp

    xcopies = []
    for q in range(4):
        rows = pl.ds(1 + 4 * q, 4)
        for d, (src_x, dst_x) in enumerate(((1, BX + 1), (BX, 0))):
            xcopies.append(
                send(
                    cells.at[src_x, rows],
                    cells.at[dst_x, rows],
                    xs_send.at[2 * q + d],
                    xs_recv.at[2 * q + d],
                    {"sx": at(n_x, sx, 2 * d - 1)},
                )
            )
    ccopies = []
    for d, (src_x, dst_x) in enumerate(((1, BX + 1), (BX, 0))):
        for f, (src_y, dst_y) in enumerate(((1, BY + 1), (BY, 0))):
            ccopies.append(
                send(
                    cells.at[src_x, src_y],
                    cells.at[dst_x, dst_y],
                    cs_send.at[2 * d + f],
                    cs_recv.at[2 * d + f],
                    {"sx": at(n_x, sx, 2 * d - 1), "sy": at(n_y, sy, 2 * f - 1)},
                )
            )

    loads[2].wait()
    relay(1)
    loads[3].wait()
    relay(2)
    ycopies = []
    for f, (src_y, dst_y) in enumerate(((1, BY + 1), (BY, 0))):
        ycopies.append(
            send(
                cells.at[pl.ds(1, BX), src_y],
                cells.at[pl.ds(1, BX), dst_y],
                ys_send.at[f],
                ys_recv.at[f],
                {"sy": at(n_y, sy, 2 * f - 1)},
            )
        )

    wcp.wait()
    zero = jnp.zeros((C, C), F32)
    for a in range(3):
        for e in range(3):
            w = [win[(a * 3 + b) * 3 + e].astype(F32) for b in range(3)]
            blocks = (
                ((w[0], w[1]), (w[2], zero)),
                ((zero, w[0]), (w[1], w[2])),
            )
            for j in range(2):
                for q in range(2):
                    toep[pl.ds(e * 128 + j * 64, 64), pl.ds(a * 256 + q * 128, 128)] = jnp.concatenate(
                        blocks[j][q], axis=1
                    ).astype(BF16)

    lane = lax.broadcasted_iota(jnp.int32, (C, 128), 1)
    row = lax.broadcasted_iota(jnp.int32, (C, 128), 0)
    eye2 = (lax.rem(lane, C) == row).astype(F32)

    def conv(pair, p):
        pieces = []
        for a in range(3):
            for i in range(4):
                pieces.append(
                    jnp.concatenate([cells[x + a, 2 * p + i] for x in PAIRS[pair]], axis=1)
                )
        d = nn(toep[...], jnp.concatenate(pieces, axis=0))
        parts = []
        for h in range(2):
            for j in range(2):
                t = [
                    d[e * 128 + j * 64 : e * 128 + j * 64 + 64, h * 128 : h * 128 + 128] for e in range(3)
                ]
                before = jnp.where(lane == 0, 0.0, pltpu.roll(t[0], 1, 1))
                after = jnp.where(lane == NZ - 1, 0.0, pltpu.roll(t[2], NZ - 1, 1))
                parts.append(before + t[1] + after)
        return parts

    def keep(pair, p, parts):
        c = centre[...]
        parts = [v - c for v in parts]
        sums[...] += (parts[0] + parts[1]) + (parts[2] + parts[3])
        hi, lo = split(jnp.concatenate(parts, axis=1))
        both = jnp.concatenate([hi, lo], axis=0)
        held[pair * 8 + p] = both
        gram[...] += lax.dot_general(both, both, (((1,), (1,)), ((), ())), preferred_element_type=F32)

    gram[...] = jnp.zeros_like(gram)
    sums[...] = jnp.zeros_like(sums)
    first = conv(0, 1)
    total = (first[0] + first[1]) + (first[2] + first[3])
    mean0 = jnp.sum(total, axis=1, keepdims=True) * (1.0 / 512)
    centre[...] = jnp.broadcast_to(mean0, (C, 128))
    keep(0, 1, first)

    def one(pair, p):
        keep(pair, p, conv(pair, p))

    def several(pair, lo, hi):
        def step(p, carry):
            one(pair, p)
            return carry

        lax.fori_loop(lo, hi, step, 0)

    several(0, 2, 7)

    def clear(cond, x, y, nx, ny):
        @pl.when(cond)
        def _():
            cells[pl.ds(x, nx), pl.ds(y, ny)] = jnp.zeros((nx, ny, C, NZ), BF16)

    x_first, x_last = sx == 0, sx == n_x - 1
    y_first, y_last = sy == 0, sy == n_y - 1
    ycopies[0].wait_recv()
    clear(y_last, 1, BY + 1, BX, 1)
    ycopies[1].wait_recv()
    clear(y_first, 1, 0, BX, 1)
    several(0, 0, 1)
    several(0, 7, 8)

    def arrive(q):
        xcopies[2 * q].wait_recv()
        clear(x_last, BX + 1, 1 + 4 * q, 1, 4)
        xcopies[2 * q + 1].wait_recv()
        clear(x_first, 0, 1 + 4 * q, 1, 4)

    arrive(0)
    arrive(1)
    several(1, 1, 3)
    arrive(2)
    several(1, 3, 5)
    arrive(3)
    several(1, 5, 7)
    for d, (x, x_edge) in enumerate(((BX + 1, x_last), (0, x_first))):
        for f, (y, y_edge) in enumerate(((BY + 1, y_last), (0, y_first))):
            ccopies[2 * d + f].wait_recv()
            clear(jnp.logical_or(x_edge, y_edge), x, y, 1, 1)
    several(1, 0, 1)
    several(1, 7, 8)

    lane32 = lane[:32]

    def pack(v):
        return jnp.where(lane32 < C, v[:32], v[32:])

    def turned(col):
        return jnp.sum(eye2 * col, axis=0, keepdims=True)

    dcol = jnp.sum(sums[...], axis=1, keepdims=True) * (1.0 / LOCAL)
    drow = turned(dcol)
    crow = turned(centre[:, 0:1])
    g = gram[:C] + gram[C:]
    g = g + pltpu.roll(g, C, 1)
    products = pack(g - LOCAL * (dcol * drow))
    mean = crow + drow
    row8 = lax.broadcasted_iota(jnp.int32, (8, 128), 0)

    def merge(products, mean, count, axis, n, me, moved, s_sem, r_sem):
        moved[me, pl.ds(0, 32)] = products
        moved[me, pl.ds(32, 8)] = jnp.where(row8 == me, mean, 0.0)
        copies = [
            send(moved.at[me], moved.at[me], s_sem.at[k - 1], r_sem.at[k - 1], {axis: at(n, me, k)})
            for k in range(1, n)
        ]
        for cp in copies:
            cp.wait_recv()
        total = moved[0]
        for i in range(1, n):
            total = total + moved[i]
        means = total[32:]
        mean = jnp.sum(means, axis=0, keepdims=True) * (1.0 / n)
        off = jnp.where(row8 < n, means - mean, 0.0)
        outer = lax.dot_general(
            off, off, (((0,), (0,)), ((), ())), precision=HIGHEST, preferred_element_type=F32
        )
        return total[:32] + count * pack(outer[:C]), mean

    products, mean = merge(products, mean, float(LOCAL), "sy", n_y, sy, moved_y, ry_send, ry_recv)
    products, mean = merge(products, mean, float(LOCAL * n_y), "batch", n_b, sb, moved_b, rb_send, rb_recv)
    products, mean = merge(products, mean, float(LOCAL * n_y * n_b), "sx", n_x, sx, moved_x, rx_send, rx_recv)

    full = jnp.concatenate([products, pltpu.roll(products, C, 1)], axis=0)[:, :C]
    eye = eye2[:, :C]
    sigma = full * (1.0 / (LOCAL * n_x * n_y * n_b)) + 1e-05 * eye
    trace = jnp.sum(jnp.sum(sigma * eye, axis=1, keepdims=True), axis=0, keepdims=True)
    t = sigma / trace
    f = None
    for turn in range(NS_ITERS):
        step = 1.5 * eye - 0.5 * t
        f = step if f is None else mm(f, step)
        if turn < NS_ITERS - 1:
            t = mm(mm(t, step), step)
    gcp.wait()
    hcp.wait()
    v = vec[...]
    gain_col = jnp.sum(eye * v[0:1], axis=1, keepdims=True)
    shift_col = jnp.sum(eye * v[1:2], axis=1, keepdims=True)
    whiten = f / jnp.sqrt(trace) * gain_col
    bias = shift_col - jnp.sum(whiten * (mean - crow)[:, :C], axis=1, keepdims=True)
    bias = jnp.broadcast_to(bias, (C, 128))
    wh, wl = split(whiten)
    mixer = jnp.concatenate([wh.astype(F32), wh.astype(F32), wl.astype(F32)], axis=1).astype(BF16)

    def mix(pair, p):
        both = held[pair * 8 + p]
        got = nn(mixer, jnp.concatenate([both, both[:C]], axis=0))
        for h in range(2):
            for j in range(2):
                k = 2 * h + j
                staged[pl.ds(PAIRS[pair][h] * BY + 2 * p + j, C, stride=BX * BY), :] = (
                    got[:, k * 128 : k * 128 + 128] + bias
                )

    writes = []
    whole = staged.reshape(C, BX * BY, NZ)
    for pair in range(2):
        for part in range(2):

            def step(p, carry):
                mix(pair, p)
                return carry

            lax.fori_loop(part * 4, part * 4 + 4, step, 0)
            for x in PAIRS[pair]:
                rows = pl.ds(x * BY + part * 8, 8)
                cp = pltpu.make_async_copy(whole.at[:, rows], out.at[:, rows], out_sem.at[len(writes)])
                cp.start()
                writes.append(cp)
    for cp in writes:
        cp.wait()
    for cp in sends:
        cp.wait_send()


def on_device(volume, conv_weight, out_gain, out_shift):
    n_x, n_y, n_b = (lax.axis_size(a) for a in ("sx", "sy", "batch"))
    weight = jnp.transpose(conv_weight, (2, 3, 4, 0, 1)).reshape(27, C, C)
    anywhere = pl.BlockSpec(memory_space=pl.ANY)
    dma = pltpu.SemaphoreType.DMA
    result = pl.pallas_call(
        lambda *refs: body((n_x, n_y, n_b), *refs),
        out_shape=jax.ShapeDtypeStruct((C, BX * BY, NZ), F32),
        in_specs=[anywhere] * 4,
        out_specs=anywhere,
        scratch_shapes=[
            pltpu.VMEM((BX, C, BY, NZ), BF16),
            pltpu.VMEM((C * BY, NZ), F32),
            pltpu.VMEM((BX + 2, BY + 2, C, NZ), BF16),
            pltpu.VMEM((27, C, C), BF16),
            pltpu.VMEM((384, 768), BF16),
            pltpu.VMEM((16, 2 * C, 512), BF16),
            pltpu.VMEM((2 * C, 2 * C), F32),
            pltpu.VMEM((C, 128), F32),
            pltpu.VMEM((C, 128), F32),
            pltpu.VMEM((n_y, 40, 128), F32),
            pltpu.VMEM((n_b, 40, 128), F32),
            pltpu.VMEM((n_x, 40, 128), F32),
            pltpu.VMEM((C * BX * BY, NZ), F32),
            pltpu.VMEM((2, C), F32),
            dma((4,)),
            dma,
            dma((2,)),
            dma((8,)),
            dma((8,)),
            dma((2,)),
            dma((2,)),
            dma((4,)),
            dma((4,)),
            dma((n_y - 1,)),
            dma((n_y - 1,)),
            dma((n_b - 1,)),
            dma((n_b - 1,)),
            dma((n_x - 1,)),
            dma((n_x - 1,)),
            dma((8,)),
        ],
        compiler_params=pltpu.CompilerParams(
            collective_id=0, has_side_effects=True, vmem_limit_bytes=40 * 1024 * 1024
        ),
    )(volume, weight, out_gain.reshape(1, C), out_shift.reshape(1, C))
    return result.reshape(1, C, BX, BY, NZ)


def solution(mesh):
    in_specs = (P("batch", None, "sx", "sy", None), P(), P(), P())
    out_specs = P("batch", None, "sx", "sy", None)
    return jax.shard_map(
        on_device, mesh=mesh, in_specs=in_specs, out_specs=out_specs, check_vma=False
    )
```

```python
import jax
import jax.numpy as jnp
from jax import lax
from jax.experimental import pallas as pl
from jax.experimental.pallas import tpu as pltpu
from jax.sharding import PartitionSpec as P

NS_ITERS = 5
C = 64
BX = 4
BY = 16
NZ = 128
LOCAL = BX * BY * NZ
MESH = pl.DeviceIdType.MESH
F32 = jnp.float32
BF16 = jnp.bfloat16
HIGHEST = lax.Precision.HIGHEST
PAIRS = ((1, 2), (0, 3))


def split(v):
    hi = v.astype(BF16)
    lo = (v - hi.astype(F32)).astype(BF16)
    return hi, lo


def nn(a, b):
    return lax.dot_general(a, b, (((1,), (0,)), ((), ())), preferred_element_type=F32)


def mm(a, b):
    ah, al = split(a)
    bh, bl = split(b)
    return nn(ah, bh) + (nn(ah, bl) + nn(al, bh))


def body(
    sizes,
    vol,
    weight,
    gain,
    shift,
    held,
    mixer,
    offset,
    vin,
    wide,
    cells,
    win,
    toep,
    gram,
    sums,
    centre,
    moved_c,
    moved_p,
    moved_x,
    vec,
    load_sem,
    wsem,
    vsem,
    xs_send,
    xs_recv,
    ys_send,
    ys_recv,
    cs_send,
    cs_recv,
    rc_send,
    rc_recv,
    rp_send,
    rp_recv,
    rx_send,
    rx_recv,
):
    n_x, n_y, n_b = sizes
    sx = lax.axis_index("sx")
    sy = lax.axis_index("sy")
    sb = lax.axis_index("batch")

    def at(n, i, k):
        return lax.rem(i + (k + n), n)

    loads = []
    for k, x in enumerate((0, 3, 1, 2)):
        cp = pltpu.make_async_copy(vol.at[0, :, x], vin.at[x], load_sem.at[k])
        cp.start()
        loads.append(cp)
    wcp = pltpu.make_async_copy(weight, win, wsem)
    wcp.start()
    gcp = pltpu.make_async_copy(gain, vec.at[pl.ds(0, 1)], vsem.at[0])
    gcp.start()
    hcp = pltpu.make_async_copy(shift, vec.at[pl.ds(1, 1)], vsem.at[1])
    hcp.start()

    n_chip = n_y // 2
    core = lax.rem(sy, 2)
    chip = sy // 2
    sibling = {"sy": sy + (1 - 2 * core)}
    others_x = [{"sx": at(n_x, sx, k)} for k in sorted(range(1, n_x), key=lambda k: -min(k, n_x - k))]
    plane = sorted(
        ((j, k) for j in range(n_chip) for k in range(n_b) if j or k),
        key=lambda o: -min(o[0], n_chip - o[0]) - min(o[1], n_b - o[1]),
    )
    others_p = [{"sy": 2 * at(n_chip, chip, j) + core, "batch": at(n_b, sb, k)} for j, k in plane]
    diagonal = [
        {"sx": at(n_x, sx, dx), "sy": at(n_y, sy, dy)} for dx in (-1, 1) for dy in (-1, 1)
    ]
    beside = {"sy": at(n_y, sy, 2 * core - 1)}

    barrier = pltpu.get_barrier_semaphore()
    greeted = [sibling, beside] + others_x + diagonal + others_p
    for device in greeted:
        pl.semaphore_signal(barrier, inc=1, device_id=device, device_id_type=MESH)

    def relay(x):
        wide[...] = vin[x].astype(F32).reshape(C * BY, NZ)
        for y in range(BY):
            cells[x + 1, y + 1] = wide[pl.ds(y, C, stride=BY), :].astype(BF16)

    loads[0].wait()
    relay(0)
    loads[1].wait()
    relay(3)
    pl.semaphore_wait(barrier, len(greeted))

    sends = []

    def send(src, dst, s_sem, r_sem, dev):
        cp = pltpu.make_async_remote_copy(
            src_ref=src, dst_ref=dst, send_sem=s_sem, recv_sem=r_sem, device_id=dev, device_id_type=MESH
        )
        cp.start()
        sends.append(cp)
        return cp

    def piece(q):
        start = 1 if q == 0 else 2 * q + 2
        stop = min(2 * q + 4, BY + 1)
        return pl.ds(start, stop - start)

    ccopies = []
    for d, (src_x, dst_x) in enumerate(((1, BX + 1), (BX, 0))):
        for f, (src_y, dst_y) in enumerate(((1, BY + 1), (BY, 0))):
            ccopies.append(
                send(
                    cells.at[src_x, src_y],
                    cells.at[dst_x, dst_y],
                    cs_send.at[2 * d + f],
                    cs_recv.at[2 * d + f],
                    {"sx": at(n_x, sx, 2 * d - 1), "sy": at(n_y, sy, 2 * f - 1)},
                )
            )

    xcopies = []
    for q in range(8):
        rows = piece(q)
        for d, (src_x, dst_x) in enumerate(((1, BX + 1), (BX, 0))):
            xcopies.append(
                send(
                    cells.at[src_x, rows],
                    cells.at[dst_x, rows],
                    xs_send.at[2 * q + d],
                    xs_recv.at[2 * q + d],
                    {"sx": at(n_x, sx, 2 * d - 1)},
                )
            )

    loads[2].wait()
    relay(1)
    loads[3].wait()
    relay(2)
    ycopies = []
    for f, (src_y, dst_y) in enumerate(((1, BY + 1), (BY, 0))):
        ycopies.append(
            send(
                cells.at[pl.ds(1, BX), src_y],
                cells.at[pl.ds(1, BX), dst_y],
                ys_send.at[f],
                ys_recv.at[f],
                {"sy": at(n_y, sy, 2 * f - 1)},
            )
        )

    wcp.wait()
    zero = jnp.zeros((C, C), F32)
    for a in range(3):
        for e in range(3):
            w = [win[(a * 3 + b) * 3 + e].astype(F32) for b in range(3)]
            blocks = (
                ((w[0], w[1]), (w[2], zero)),
                ((zero, w[0]), (w[1], w[2])),
            )
            for j in range(2):
                for q in range(2):
                    toep[pl.ds(e * 128 + j * 64, 64), pl.ds(a * 256 + q * 128, 128)] = jnp.concatenate(
                        blocks[j][q], axis=1
                    ).astype(BF16)

    lane = lax.broadcasted_iota(jnp.int32, (C, 128), 1)
    row = lax.broadcasted_iota(jnp.int32, (C, 128), 0)
    eye2 = (lax.rem(lane, C) == row).astype(F32)

    def conv(pair, p):
        pieces = []
        for a in range(3):
            for i in range(4):
                pieces.append(
                    jnp.concatenate([cells[x + a, 2 * p + i] for x in PAIRS[pair]], axis=1)
                )
        d = nn(toep[...], jnp.concatenate(pieces, axis=0))
        parts = []
        for h in range(2):
            for j in range(2):
                t = [
                    d[e * 128 + j * 64 : e * 128 + j * 64 + 64, h * 128 : h * 128 + 128] for e in range(3)
                ]
                before = jnp.where(lane == 0, 0.0, pltpu.roll(t[0], 1, 1))
                after = jnp.where(lane == NZ - 1, 0.0, pltpu.roll(t[2], NZ - 1, 1))
                parts.append(before + t[1] + after)
        return parts

    def keep(pair, p, parts):
        c = centre[...]
        parts = [v - c for v in parts]
        sums[...] += (parts[0] + parts[1]) + (parts[2] + parts[3])
        hi, lo = split(jnp.concatenate(parts, axis=1))
        both = jnp.concatenate([hi, lo], axis=0)
        held[pair * 8 + p] = both
        gram[...] += lax.dot_general(both, both, (((1,), (1,)), ((), ())), preferred_element_type=F32)

    gram[...] = jnp.zeros_like(gram)
    sums[...] = jnp.zeros_like(sums)
    first = conv(0, 1)
    total = (first[0] + first[1]) + (first[2] + first[3])
    mean0 = jnp.sum(total, axis=1, keepdims=True) * (1.0 / 512)
    centre[...] = jnp.broadcast_to(mean0, (C, 128))
    keep(0, 1, first)

    def one(pair, p):
        keep(pair, p, conv(pair, p))

    def several(pair, lo, hi):
        for p in range(lo, hi):
            one(pair, p)

    several(0, 2, 7)

    def clear(cond, x, y, nx, ny):
        @pl.when(cond)
        def _():
            cells[pl.ds(x, nx), pl.ds(y, ny)] = jnp.zeros((nx, ny, C, NZ), BF16)

    x_first, x_last = sx == 0, sx == n_x - 1
    y_first, y_last = sy == 0, sy == n_y - 1
    ycopies[0].wait_recv()
    clear(y_last, 1, BY + 1, BX, 1)
    ycopies[1].wait_recv()
    clear(y_first, 1, 0, BX, 1)
    several(0, 0, 1)
    several(0, 7, 8)

    def corner(f, y, y_edge):
        for d, (x, x_edge) in enumerate(((BX + 1, x_last), (0, x_first))):
            ccopies[2 * d + f].wait_recv()
            clear(jnp.logical_or(x_edge, y_edge), x, y, 1, 1)

    corner(1, 0, y_first)
    corner(0, BY + 1, y_last)
    for q in range(8):
        rows = piece(q)
        xcopies[2 * q].wait_recv()
        clear(x_last, BX + 1, rows.start, 1, rows.size)
        xcopies[2 * q + 1].wait_recv()
        clear(x_first, 0, rows.start, 1, rows.size)
        one(1, q)

    def turned(col):
        return jnp.sum(eye2 * col, axis=0, keepdims=True)

    H = C // 2
    lane32, row32 = lane[:H], row[:H]
    low = lax.rem(lane32, C)

    def pack(v):
        top = v[:H]
        last = pltpu.roll(v[H:], 128 - H, 1)
        mixed = jnp.where(jnp.logical_and(low < H, row32 > low), last, top)
        diag = jnp.sum(jnp.where(low == row32, last, 0.0), axis=0, keepdims=True)
        return jnp.where(lane32[:16] < C, mixed[:16], mixed[16:]), diag

    dcol = jnp.sum(sums[...], axis=1, keepdims=True) * (1.0 / LOCAL)
    drow = turned(dcol)
    crow = turned(centre[:, 0:1])
    g = gram[:C] + gram[C:]
    g = g + pltpu.roll(g, C, 1)
    products, diag = pack(g - LOCAL * (dcol * drow))
    mean = crow + drow
    lane1 = lane[:1]

    def merge(products, diag, mean, count, n, me, others, moved, s_sem, r_sem):
        high = moved.shape[1] - 16
        rows = row[:high]
        line = jnp.where(lane1 < C, mean, jnp.where(lane1 < C + H, diag, 0.0))
        moved[me, pl.ds(0, 16)] = products
        moved[me, pl.ds(16, high)] = jnp.where(rows == me, line, 0.0)
        copies = [
            send(moved.at[me], moved.at[me], s_sem.at[k], r_sem.at[k], device)
            for k, device in enumerate(others)
        ]
        for cp in copies:
            cp.wait_recv()
        total = moved[0]
        for i in range(1, n):
            total = total + moved[i]
        means = total[16:]
        line = jnp.sum(means, axis=0, keepdims=True)
        mean = jnp.where(lane1 < C, line * (1.0 / n), 0.0)
        off = jnp.where(jnp.logical_and(rows < n, lane[:high] < C), means - mean, 0.0)
        off = off + pltpu.roll(off, C, 1)
        outer = lax.dot_general(
            off, off, (((0,), (0,)), ((), ())), precision=HIGHEST, preferred_element_type=F32
        )
        more, more_diag = pack(outer[:C])
        return total[:16] + count * more, line + count * more_diag, mean + pltpu.roll(mean, C, 1)

    count = float(LOCAL)
    state = merge(products, diag, mean, count, 2, core, [sibling], moved_c, rc_send, rc_recv)
    count *= 2
    state = merge(
        *state, count, n_chip * n_b, chip * n_b + sb, others_p, moved_p, rp_send, rp_recv
    )
    count *= n_chip * n_b
    products, diag, mean = merge(*state, count, n_x, sx, others_x, moved_x, rx_send, rx_recv)

    half = jnp.concatenate([products, pltpu.roll(products, C, 1)], axis=0)
    across = jnp.concatenate([half, jnp.zeros((128 - H, 128), F32)], axis=0).T
    upper = jnp.where(jnp.logical_and(lane32 < H, row32 > lane32), across[:H], half)
    last = pltpu.roll(jnp.where(row32 > lane32, half, across[:H]), H, 1)
    last = jnp.where(lane32 == row32 + H, pltpu.roll(diag, 128 - H, 1), last)
    lower = jnp.where(lane32 < H, across[H:C], last)
    full = jnp.concatenate([upper, lower], axis=0)[:, :C]
    eye = eye2[:, :C]
    sigma = full * (1.0 / (LOCAL * n_x * n_y * n_b)) + 1e-05 * eye
    trace = jnp.sum(jnp.sum(sigma * eye, axis=1, keepdims=True), axis=0, keepdims=True)
    t = sigma / trace
    f = None
    for turn in range(NS_ITERS):
        step = 1.5 * eye - 0.5 * t
        f = step if f is None else mm(f, step)
        if turn < NS_ITERS - 1:
            t = mm(mm(t, step), step)
    gcp.wait()
    hcp.wait()
    v = vec[...]
    gain_col = jnp.sum(eye * v[0:1], axis=1, keepdims=True)
    shift_col = jnp.sum(eye * v[1:2], axis=1, keepdims=True)
    whiten = f / jnp.sqrt(trace) * gain_col
    bias = shift_col - jnp.sum(whiten * (mean - crow)[:, :C], axis=1, keepdims=True)
    offset[...] = jnp.broadcast_to(bias, (C, 128))
    wh, wl = split(whiten)
    mixer[...] = jnp.concatenate([wh.astype(F32), wh.astype(F32), wl.astype(F32)], axis=1).astype(BF16)
    for cp in sends:
        cp.wait_send()


def mix_body(held, mixer, offset, out, staged, sem):
    writes = []
    whole = staged.reshape(C, BX * BY, NZ)
    bias = offset[...]
    for pair in range(2):
        for part in range(2):
            for p in range(part * 4, part * 4 + 4):
                both = held[pair * 8 + p]
                got = nn(mixer[...], jnp.concatenate([both, both[:C]], axis=0))
                for h in range(2):
                    for j in range(2):
                        k = 2 * h + j
                        staged[pl.ds(PAIRS[pair][h] * BY + 2 * p + j, C, stride=BX * BY), :] = (
                            got[:, k * 128 : k * 128 + 128] + bias
                        )
            for x in PAIRS[pair]:
                rows = pl.ds(x * BY + part * 8, 8)
                cp = pltpu.make_async_copy(whole.at[:, rows], out.at[:, rows], sem.at[len(writes)])
                cp.start()
                writes.append(cp)
    for cp in writes:
        cp.wait()


def on_device(volume, conv_weight, out_gain, out_shift):
    n_x, n_y, n_b = (lax.axis_size(a) for a in ("sx", "sy", "batch"))
    weight = jnp.transpose(conv_weight, (2, 3, 4, 0, 1)).reshape(27, C, C)
    anywhere = pl.BlockSpec(memory_space=pl.ANY)
    inside = pl.BlockSpec(memory_space=pltpu.VMEM)
    dma = pltpu.SemaphoreType.DMA
    n_p = n_y // 2 * n_b
    operands = (volume, weight, out_gain.reshape(1, C), out_shift.reshape(1, C))
    held, mixer, offset = pl.pallas_call(
        lambda *refs: body((n_x, n_y, n_b), *refs),
        out_shape=[
            jax.ShapeDtypeStruct((16, 2 * C, 512), BF16),
            jax.ShapeDtypeStruct((C, 3 * C), BF16),
            jax.ShapeDtypeStruct((C, 128), F32),
        ],
        in_specs=[anywhere] * 4,
        out_specs=[inside] * 3,
        scratch_shapes=[
            pltpu.VMEM((BX, C, BY, NZ), BF16),
            pltpu.VMEM((C * BY, NZ), F32),
            pltpu.VMEM((BX + 2, BY + 2, C, NZ), BF16),
            pltpu.VMEM((27, C, C), BF16),
            pltpu.VMEM((384, 768), BF16),
            pltpu.VMEM((2 * C, 2 * C), F32),
            pltpu.VMEM((C, 128), F32),
            pltpu.VMEM((C, 128), F32),
            pltpu.VMEM((2, 24, 128), F32),
            pltpu.VMEM((n_p, 32, 128), F32),
            pltpu.VMEM((n_x, 24, 128), F32),
            pltpu.VMEM((2, C), F32),
            dma((4,)),
            dma,
            dma((2,)),
            dma((16,)),
            dma((16,)),
            dma((2,)),
            dma((2,)),
            dma((4,)),
            dma((4,)),
            dma((1,)),
            dma((1,)),
            dma((n_p - 1,)),
            dma((n_p - 1,)),
            dma((n_x - 1,)),
            dma((n_x - 1,)),
        ],
        compiler_params=pltpu.CompilerParams(
            collective_id=0, has_side_effects=True, vmem_limit_bytes=40 * 1024 * 1024
        ),
    )(*(pltpu.with_memory_space_constraint(v, pltpu.HBM) for v in operands))
    result = pl.pallas_call(
        mix_body,
        out_shape=jax.ShapeDtypeStruct((C, BX * BY, NZ), F32),
        in_specs=[inside] * 3,
        out_specs=anywhere,
        scratch_shapes=[pltpu.VMEM((C * BX * BY, NZ), F32), dma((8,))],
        compiler_params=pltpu.CompilerParams(vmem_limit_bytes=40 * 1024 * 1024),
    )(held, mixer, offset)
    return result.reshape(1, C, BX, BY, NZ)


def solution(mesh):
    in_specs = (P("batch", None, "sx", "sy", None), P(), P(), P())
    out_specs = P("batch", None, "sx", "sy", None)
    return jax.shard_map(
        on_device, mesh=mesh, in_specs=in_specs, out_specs=out_specs, check_vma=False
    )
```

```python
import jax
import jax.numpy as jnp
from jax import lax
from jax.experimental import pallas as pl
from jax.experimental.pallas import tpu as pltpu
from jax.sharding import PartitionSpec as P

NS_ITERS = 5
C = 64
BX = 4
BY = 16
NZ = 128
LOCAL = BX * BY * NZ
MESH = pl.DeviceIdType.MESH
F32 = jnp.float32
BF16 = jnp.bfloat16
HIGHEST = lax.Precision.HIGHEST
LAST = (1, 2, 3, 4, 5, 6, 7, 8)
PAIRS = ((1, 2), (0, 3))


def split(v):
    hi = v.astype(BF16)
    lo = (v - hi.astype(F32)).astype(BF16)
    return hi, lo


def nn(a, b):
    return lax.dot_general(a, b, (((1,), (0,)), ((), ())), preferred_element_type=F32)


def mm(a, b):
    ah, al = split(a)
    bh, bl = split(b)
    return nn(ah, bh) + (nn(ah, bl) + nn(al, bh))


def body(
    sizes,
    vol,
    weight,
    gain,
    shift,
    held,
    mixer,
    offset,
    vin,
    wide,
    cells,
    win,
    toep,
    gram,
    sums,
    centre,
    moved_c,
    moved_p,
    moved_x,
    vec,
    load_sem,
    wsem,
    vsem,
    xs_send,
    xs_recv,
    ys_send,
    ys_recv,
    cs_send,
    cs_recv,
    rc_send,
    rc_recv,
    rp_send,
    rp_recv,
    rx_send,
    rx_recv,
):
    n_x, n_y, n_b = sizes
    sx = lax.axis_index("sx")
    sy = lax.axis_index("sy")
    sb = lax.axis_index("batch")

    def at(n, i, k):
        return lax.rem(i + (k + n), n)

    loads = []
    for k, x in enumerate((0, 3, 1, 2)):
        cp = pltpu.make_async_copy(vol.at[0, :, x], vin.at[x], load_sem.at[k])
        cp.start()
        loads.append(cp)
    wcp = pltpu.make_async_copy(weight, win, wsem)
    wcp.start()
    gcp = pltpu.make_async_copy(gain, vec.at[pl.ds(0, 1)], vsem.at[0])
    gcp.start()
    hcp = pltpu.make_async_copy(shift, vec.at[pl.ds(1, 1)], vsem.at[1])
    hcp.start()

    n_chip = n_y // 2
    core = lax.rem(sy, 2)
    chip = sy // 2
    sibling = {"sy": sy + (1 - 2 * core)}
    others_x = [{"sx": at(n_x, sx, k)} for k in sorted(range(1, n_x), key=lambda k: -min(k, n_x - k))]
    plane = sorted(
        ((j, k) for j in range(n_chip) for k in range(n_b) if j or k),
        key=lambda o: -min(o[0], n_chip - o[0]) - min(o[1], n_b - o[1]),
    )
    others_p = [{"sy": 2 * at(n_chip, chip, j) + core, "batch": at(n_b, sb, k)} for j, k in plane]
    diagonal = [
        {"sx": at(n_x, sx, dx), "sy": at(n_y, sy, dy)} for dx in (-1, 1) for dy in (-1, 1)
    ]
    beside = {"sy": at(n_y, sy, 2 * core - 1)}

    barrier = pltpu.get_barrier_semaphore()
    greeted = others_x[::-1] + diagonal + [beside, sibling] + others_p
    for device in greeted:
        pl.semaphore_signal(barrier, inc=1, device_id=device, device_id_type=MESH)

    def relay(x):
        wide[...] = vin[x].astype(F32).reshape(C * BY, NZ)
        for y in range(BY):
            cells[x + 1, y + 1] = wide[pl.ds(y, C, stride=BY), :].astype(BF16)

    loads[0].wait()
    relay(0)
    loads[1].wait()
    relay(3)
    pl.semaphore_wait(barrier, len(greeted))

    sends = []

    def send(src, dst, s_sem, r_sem, dev):
        cp = pltpu.make_async_remote_copy(
            src_ref=src, dst_ref=dst, send_sem=s_sem, recv_sem=r_sem, device_id=dev, device_id_type=MESH
        )
        cp.start()
        sends.append(cp)
        return cp

    def piece(q):
        start = 1 if q == 0 else 2 * LAST[q - 1] + 2
        stop = min(2 * LAST[q] + 2, BY + 1)
        return pl.ds(start, stop - start)

    ccopies = []
    for d, (src_x, dst_x) in enumerate(((1, BX + 1), (BX, 0))):
        for f, (src_y, dst_y) in enumerate(((1, BY + 1), (BY, 0))):
            ccopies.append(
                send(
                    cells.at[src_x, src_y],
                    cells.at[dst_x, dst_y],
                    cs_send.at[2 * d + f],
                    cs_recv.at[2 * d + f],
                    {"sx": at(n_x, sx, 2 * d - 1), "sy": at(n_y, sy, 2 * f - 1)},
                )
            )

    xcopies = []
    for q in range(len(LAST)):
        rows = piece(q)
        for d, (src_x, dst_x) in enumerate(((1, BX + 1), (BX, 0))):
            xcopies.append(
                send(
                    cells.at[src_x, rows],
                    cells.at[dst_x, rows],
                    xs_send.at[2 * q + d],
                    xs_recv.at[2 * q + d],
                    {"sx": at(n_x, sx, 2 * d - 1)},
                )
            )

    loads[2].wait()
    relay(1)
    loads[3].wait()
    relay(2)
    ycopies = []
    for f, (src_y, dst_y) in enumerate(((1, BY + 1), (BY, 0))):
        ycopies.append(
            send(
                cells.at[pl.ds(1, BX), src_y],
                cells.at[pl.ds(1, BX), dst_y],
                ys_send.at[f],
                ys_recv.at[f],
                {"sy": at(n_y, sy, 2 * f - 1)},
            )
        )

    wcp.wait()
    zero = jnp.zeros((C, C), F32)
    for a in range(3):
        for e in range(3):
            w = [win[(a * 3 + b) * 3 + e].astype(F32) for b in range(3)]
            blocks = (
                ((w[0], w[1]), (w[2], zero)),
                ((zero, w[0]), (w[1], w[2])),
            )
            for j in range(2):
                for q in range(2):
                    toep[pl.ds(e * 128 + j * 64, 64), pl.ds(a * 256 + q * 128, 128)] = jnp.concatenate(
                        blocks[j][q], axis=1
                    ).astype(BF16)

    lane = lax.broadcasted_iota(jnp.int32, (C, 128), 1)
    row = lax.broadcasted_iota(jnp.int32, (C, 128), 0)
    eye2 = (lax.rem(lane, C) == row).astype(F32)

    def conv(pair, p):
        pieces = []
        for a in range(3):
            for i in range(4):
                pieces.append(
                    jnp.concatenate([cells[x + a, 2 * p + i] for x in PAIRS[pair]], axis=1)
                )
        d = nn(toep[...], jnp.concatenate(pieces, axis=0))
        parts = []
        for h in range(2):
            for j in range(2):
                t = [
                    d[e * 128 + j * 64 : e * 128 + j * 64 + 64, h * 128 : h * 128 + 128] for e in range(3)
                ]
                before = jnp.where(lane == 0, 0.0, pltpu.roll(t[0], 1, 1))
                after = jnp.where(lane == NZ - 1, 0.0, pltpu.roll(t[2], NZ - 1, 1))
                parts.append(before + t[1] + after)
        return parts

    def keep(pair, p, parts):
        c = centre[...]
        parts = [v - c for v in parts]
        sums[...] += (parts[0] + parts[1]) + (parts[2] + parts[3])
        hi, lo = split(jnp.concatenate(parts, axis=1))
        both = jnp.concatenate([hi, lo], axis=0)
        held[pair * 8 + p] = both
        gram[...] += lax.dot_general(both, both, (((1,), (1,)), ((), ())), preferred_element_type=F32)

    gram[...] = jnp.zeros_like(gram)
    sums[...] = jnp.zeros_like(sums)
    first = conv(0, 1)
    total = (first[0] + first[1]) + (first[2] + first[3])
    mean0 = jnp.sum(total, axis=1, keepdims=True) * (1.0 / 512)
    centre[...] = jnp.broadcast_to(mean0, (C, 128))
    keep(0, 1, first)

    def one(pair, p):
        keep(pair, p, conv(pair, p))

    def several(pair, lo, hi):
        for p in range(lo, hi):
            one(pair, p)

    several(0, 2, 7)

    def clear(cond, x, y, nx, ny):
        @pl.when(cond)
        def _():
            cells[pl.ds(x, nx), pl.ds(y, ny)] = jnp.zeros((nx, ny, C, NZ), BF16)

    x_first, x_last = sx == 0, sx == n_x - 1
    y_first, y_last = sy == 0, sy == n_y - 1
    ycopies[0].wait_recv()
    clear(y_last, 1, BY + 1, BX, 1)
    ycopies[1].wait_recv()
    clear(y_first, 1, 0, BX, 1)
    several(0, 0, 1)
    several(0, 7, 8)

    def corner(f, y, y_edge):
        for d, (x, x_edge) in enumerate(((BX + 1, x_last), (0, x_first))):
            ccopies[2 * d + f].wait_recv()
            clear(jnp.logical_or(x_edge, y_edge), x, y, 1, 1)

    corner(1, 0, y_first)
    corner(0, BY + 1, y_last)
    for q in range(len(LAST)):
        rows = piece(q)
        xcopies[2 * q].wait_recv()
        clear(x_last, BX + 1, rows.start, 1, rows.size)
        xcopies[2 * q + 1].wait_recv()
        clear(x_first, 0, rows.start, 1, rows.size)
        several(1, LAST[q - 1] if q else 0, LAST[q])

    def turned(col):
        return jnp.sum(eye2 * col, axis=0, keepdims=True)

    H = C // 2
    lane32, row32 = lane[:H], row[:H]
    low = lax.rem(lane32, C)

    def pack(v):
        top = v[:H]
        last = pltpu.roll(v[H:], 128 - H, 1)
        mixed = jnp.where(jnp.logical_and(low < H, row32 > low), last, top)
        diag = jnp.sum(jnp.where(low == row32, last, 0.0), axis=0, keepdims=True)
        return jnp.where(lane32[:16] < C, mixed[:16], mixed[16:]), diag

    dcol = jnp.sum(sums[...], axis=1, keepdims=True) * (1.0 / LOCAL)
    drow = turned(dcol)
    crow = turned(centre[:, 0:1])
    g = gram[:C] + gram[C:]
    g = g + pltpu.roll(g, C, 1)
    products, diag = pack(g - LOCAL * (dcol * drow))
    mean = crow + drow
    lane1 = lane[:1]

    def merge(products, diag, mean, count, n, me, others, moved, s_sem, r_sem):
        high = moved.shape[1] - 16
        rows = row[:high]
        line = jnp.where(lane1 < C, mean, jnp.where(lane1 < C + H, diag, 0.0))
        moved[me, pl.ds(0, 16)] = products
        moved[me, pl.ds(16, high)] = jnp.where(rows == me, line, 0.0)
        copies = [
            send(moved.at[me], moved.at[me], s_sem.at[k], r_sem.at[k], device)
            for k, device in enumerate(others)
        ]
        for cp in copies:
            cp.wait_recv()
        total = moved[0]
        for i in range(1, n):
            total = total + moved[i]
        means = total[16:]
        line = jnp.sum(means, axis=0, keepdims=True)
        mean = jnp.where(lane1 < C, line * (1.0 / n), 0.0)
        off = jnp.where(jnp.logical_and(rows < n, lane[:high] < C), means - mean, 0.0)
        off = off + pltpu.roll(off, C, 1)
        outer = lax.dot_general(
            off, off, (((0,), (0,)), ((), ())), precision=HIGHEST, preferred_element_type=F32
        )
        more, more_diag = pack(outer[:C])
        return total[:16] + count * more, line + count * more_diag, mean + pltpu.roll(mean, C, 1)

    count = float(LOCAL)
    state = merge(products, diag, mean, count, 2, core, [sibling], moved_c, rc_send, rc_recv)
    count *= 2
    state = merge(
        *state, count, n_chip * n_b, chip * n_b + sb, others_p, moved_p, rp_send, rp_recv
    )
    count *= n_chip * n_b
    products, diag, mean = merge(*state, count, n_x, sx, others_x, moved_x, rx_send, rx_recv)

    half = jnp.concatenate([products, pltpu.roll(products, C, 1)], axis=0)
    across = jnp.concatenate([half, jnp.zeros((128 - H, 128), F32)], axis=0).T
    upper = jnp.where(jnp.logical_and(lane32 < H, row32 > lane32), across[:H], half)
    last = pltpu.roll(jnp.where(row32 > lane32, half, across[:H]), H, 1)
    last = jnp.where(lane32 == row32 + H, pltpu.roll(diag, 128 - H, 1), last)
    lower = jnp.where(lane32 < H, across[H:C], last)
    full = jnp.concatenate([upper, lower], axis=0)[:, :C]
    eye = eye2[:, :C]
    sigma = full * (1.0 / (LOCAL * n_x * n_y * n_b)) + 1e-05 * eye
    trace = jnp.sum(jnp.sum(sigma * eye, axis=1, keepdims=True), axis=0, keepdims=True)
    t = sigma / trace
    f = None
    for turn in range(NS_ITERS):
        step = 1.5 * eye - 0.5 * t
        f = step if f is None else mm(f, step)
        if turn < NS_ITERS - 1:
            t = mm(mm(t, step), step)
    gcp.wait()
    hcp.wait()
    v = vec[...]
    gain_col = jnp.sum(eye * v[0:1], axis=1, keepdims=True)
    shift_col = jnp.sum(eye * v[1:2], axis=1, keepdims=True)
    whiten = f / jnp.sqrt(trace) * gain_col
    bias = shift_col - jnp.sum(whiten * (mean - crow)[:, :C], axis=1, keepdims=True)
    offset[...] = jnp.broadcast_to(bias, (C, 128))
    wh, wl = split(whiten)
    mixer[...] = jnp.concatenate([wh.astype(F32), wh.astype(F32), wl.astype(F32)], axis=1).astype(BF16)
    for cp in sends:
        cp.wait_send()


def mix_body(held, mixer, offset, out, staged, sem):
    bias = offset[...]
    for pair in range(2):
        for p in range(8):
            both = held[pair * 8 + p]
            got = nn(mixer[...], jnp.concatenate([both, both[:C]], axis=0))
            for h in range(2):
                for j in range(2):
                    k = 2 * h + j
                    place = PAIRS[pair][h] * BY + 2 * p + j
                    staged[place] = got[:, k * 128 : k * 128 + 128] + bias
                    pltpu.make_async_copy(staged.at[place], out.at[:, place], sem).start()
    pltpu.make_async_copy(staged, out, sem).wait()


def on_device(volume, conv_weight, out_gain, out_shift):
    n_x, n_y, n_b = (lax.axis_size(a) for a in ("sx", "sy", "batch"))
    weight = jnp.transpose(conv_weight, (2, 3, 4, 0, 1)).reshape(27, C, C)
    anywhere = pl.BlockSpec(memory_space=pl.ANY)
    inside = pl.BlockSpec(memory_space=pltpu.VMEM)
    dma = pltpu.SemaphoreType.DMA
    n_p = n_y // 2 * n_b
    operands = (volume, weight, out_gain.reshape(1, C), out_shift.reshape(1, C))
    held, mixer, offset = pl.pallas_call(
        lambda *refs: body((n_x, n_y, n_b), *refs),
        out_shape=[
            jax.ShapeDtypeStruct((16, 2 * C, 512), BF16),
            jax.ShapeDtypeStruct((C, 3 * C), BF16),
            jax.ShapeDtypeStruct((C, 128), F32),
        ],
        in_specs=[anywhere] * 4,
        out_specs=[inside] * 3,
        scratch_shapes=[
            pltpu.VMEM((BX, C, BY, NZ), BF16),
            pltpu.VMEM((C * BY, NZ), F32),
            pltpu.VMEM((BX + 2, BY + 2, C, NZ), BF16),
            pltpu.VMEM((27, C, C), BF16),
            pltpu.VMEM((384, 768), BF16),
            pltpu.VMEM((2 * C, 2 * C), F32),
            pltpu.VMEM((C, 128), F32),
            pltpu.VMEM((C, 128), F32),
            pltpu.VMEM((2, 24, 128), F32),
            pltpu.VMEM((n_p, 32, 128), F32),
            pltpu.VMEM((n_x, 24, 128), F32),
            pltpu.VMEM((2, C), F32),
            dma((4,)),
            dma,
            dma((2,)),
            dma((2 * len(LAST),)),
            dma((2 * len(LAST),)),
            dma((2,)),
            dma((2,)),
            dma((4,)),
            dma((4,)),
            dma((1,)),
            dma((1,)),
            dma((n_p - 1,)),
            dma((n_p - 1,)),
            dma((n_x - 1,)),
            dma((n_x - 1,)),
        ],
        compiler_params=pltpu.CompilerParams(
            collective_id=0, has_side_effects=True, vmem_limit_bytes=40 * 1024 * 1024
        ),
    )(*(pltpu.with_memory_space_constraint(v, pltpu.HBM) for v in operands))
    result = pl.pallas_call(
        mix_body,
        out_shape=jax.ShapeDtypeStruct((C, BX * BY, NZ), F32),
        in_specs=[inside] * 3,
        out_specs=anywhere,
        scratch_shapes=[pltpu.VMEM((BX * BY, C, NZ), F32), dma],
        compiler_params=pltpu.CompilerParams(vmem_limit_bytes=40 * 1024 * 1024),
    )(held, mixer, offset)
    return result.reshape(1, C, BX, BY, NZ)


def solution(mesh):
    in_specs = (P("batch", None, "sx", "sy", None), P(), P(), P())
    out_specs = P("batch", None, "sx", "sy", None)
    return jax.shard_map(
        on_device, mesh=mesh, in_specs=in_specs, out_specs=out_specs, check_vma=False
    )
```

```python
import jax
import jax.numpy as jnp
from jax import lax
from jax.experimental import pallas as pl
from jax.experimental.pallas import tpu as pltpu
from jax.sharding import PartitionSpec as P

NS_ITERS = 5
C = 64
BX = 4
BY = 16
NZ = 128
LOCAL = BX * BY * NZ
MESH = pl.DeviceIdType.MESH
F32 = jnp.float32
BF16 = jnp.bfloat16
LAST = (1, 2, 3, 4, 5, 6, 7, 8)
PAIRS = ((1, 2), (0, 3))


def split(v):
    hi = v.astype(BF16)
    lo = (v - hi.astype(F32)).astype(BF16)
    return hi, lo


def nn(a, b):
    return lax.dot_general(a, b, (((1,), (0,)), ((), ())), preferred_element_type=F32)


def mm(a, b):
    ah, al = split(a)
    bh, bl = split(b)
    return nn(ah, bh) + (nn(ah, bl) + nn(al, bh))


def body(
    sizes,
    vol,
    weight,
    gain,
    shift,
    held,
    mixer,
    offset,
    vin,
    wide,
    cells,
    win,
    toep,
    gram,
    sums,
    centre,
    moved_c,
    moved_p,
    moved_x,
    vec,
    load_sem,
    wsem,
    vsem,
    xs_send,
    xs_recv,
    ys_send,
    ys_recv,
    cs_send,
    cs_recv,
    rc_send,
    rc_recv,
    rp_send,
    rp_recv,
    rx_send,
    rx_recv,
    known,
):
    n_x, n_y, n_b = sizes
    sx = lax.axis_index("sx")
    sy = lax.axis_index("sy")
    sb = lax.axis_index("batch")

    def at(n, i, k):
        return lax.rem(i + (k + n), n)

    loads = []
    for k, x in enumerate((0, 3, 1, 2)):
        cp = pltpu.make_async_copy(vol.at[0, :, x], vin.at[x], load_sem.at[k])
        cp.start()
        loads.append(cp)
    wcp = pltpu.make_async_copy(weight, win, wsem)
    wcp.start()
    gcp = pltpu.make_async_copy(gain, vec.at[pl.ds(0, 1)], vsem.at[0])
    gcp.start()
    hcp = pltpu.make_async_copy(shift, vec.at[pl.ds(1, 1)], vsem.at[1])
    hcp.start()

    n_chip = n_y // 2
    core = lax.rem(sy, 2)
    chip = sy // 2
    sibling = {"sy": sy + (1 - 2 * core)}
    others_x = [{"sx": at(n_x, sx, k)} for k in sorted(range(1, n_x), key=lambda k: -min(k, n_x - k))]
    plane = sorted(
        ((j, k) for j in range(n_chip) for k in range(n_b) if j or k),
        key=lambda o: -min(o[0], n_chip - o[0]) - min(o[1], n_b - o[1]),
    )
    others_p = [{"sy": 2 * at(n_chip, chip, j) + core, "batch": at(n_b, sb, k)} for j, k in plane]
    diagonal = [
        {"sx": at(n_x, sx, dx), "sy": at(n_y, sy, dy)} for dx in (-1, 1) for dy in (-1, 1)
    ]
    beside = {"sy": at(n_y, sy, 2 * core - 1)}

    barrier = pltpu.get_barrier_semaphore()
    near_x = [{"sx": at(n_x, sx, k)} for k in (-1, 1)]
    near_y = [{"sy": at(n_y, sy, k)} for k in (-2, 2)]
    near_b = [{"batch": at(n_b, sb, k)} for k in (-1, 1)]
    greeted = near_x + diagonal + [beside, sibling] + near_y + near_b
    for device in greeted:
        pl.semaphore_signal(barrier, inc=1, device_id=device, device_id_type=MESH)

    def tell(k):
        for device in near_x:
            pl.semaphore_signal(known.at[k, 0], inc=1, device_id=device, device_id_type=MESH)
        for device in near_b if k else near_y:
            pl.semaphore_signal(known.at[k, 1], inc=1, device_id=device, device_id_type=MESH)

    def hear(k):
        pl.semaphore_wait(known.at[k, 0], 2)
        pl.semaphore_wait(known.at[k, 1], 2)

    def relay(x):
        wide[...] = vin[x].astype(F32).reshape(C * BY, NZ)
        for y in range(BY):
            cells[x + 1, y + 1] = wide[pl.ds(y, C, stride=BY), :].astype(BF16)

    loads[0].wait()
    relay(0)
    loads[1].wait()
    relay(3)
    pl.semaphore_wait(barrier, len(greeted))

    sends = []

    def send(src, dst, s_sem, r_sem, dev):
        cp = pltpu.make_async_remote_copy(
            src_ref=src, dst_ref=dst, send_sem=s_sem, recv_sem=r_sem, device_id=dev, device_id_type=MESH
        )
        cp.start()
        sends.append(cp)
        return cp

    def piece(q):
        start = 1 if q == 0 else 2 * LAST[q - 1] + 2
        stop = min(2 * LAST[q] + 2, BY + 1)
        return pl.ds(start, stop - start)

    ccopies = []
    for d, (src_x, dst_x) in enumerate(((1, BX + 1), (BX, 0))):
        for f, (src_y, dst_y) in enumerate(((1, BY + 1), (BY, 0))):
            ccopies.append(
                send(
                    cells.at[src_x, src_y],
                    cells.at[dst_x, dst_y],
                    cs_send.at[2 * d + f],
                    cs_recv.at[2 * d + f],
                    {"sx": at(n_x, sx, 2 * d - 1), "sy": at(n_y, sy, 2 * f - 1)},
                )
            )

    xcopies = []
    for q in range(len(LAST)):
        rows = piece(q)
        for d, (src_x, dst_x) in enumerate(((1, BX + 1), (BX, 0))):
            xcopies.append(
                send(
                    cells.at[src_x, rows],
                    cells.at[dst_x, rows],
                    xs_send.at[2 * q + d],
                    xs_recv.at[2 * q + d],
                    {"sx": at(n_x, sx, 2 * d - 1)},
                )
            )

    loads[2].wait()
    relay(1)
    loads[3].wait()
    relay(2)
    ycopies = []
    for f, (src_y, dst_y) in enumerate(((1, BY + 1), (BY, 0))):
        ycopies.append(
            send(
                cells.at[pl.ds(1, BX), src_y],
                cells.at[pl.ds(1, BX), dst_y],
                ys_send.at[f],
                ys_recv.at[f],
                {"sy": at(n_y, sy, 2 * f - 1)},
            )
        )

    tell(0)
    wcp.wait()
    zero = jnp.zeros((C, C), F32)
    for a in range(3):
        for e in range(3):
            w = [win[(a * 3 + b) * 3 + e].astype(F32) for b in range(3)]
            blocks = (
                ((w[0], w[1]), (w[2], zero)),
                ((zero, w[0]), (w[1], w[2])),
            )
            for j in range(2):
                for q in range(2):
                    toep[pl.ds(e * 128 + j * 64, 64), pl.ds(a * 256 + q * 128, 128)] = jnp.concatenate(
                        blocks[j][q], axis=1
                    ).astype(BF16)

    lane = lax.broadcasted_iota(jnp.int32, (C, 128), 1)
    row = lax.broadcasted_iota(jnp.int32, (C, 128), 0)
    eye2 = (lax.rem(lane, C) == row).astype(F32)

    def conv(pair, p):
        pieces = []
        for a in range(3):
            for i in range(4):
                pieces.append(
                    jnp.concatenate([cells[x + a, 2 * p + i] for x in PAIRS[pair]], axis=1)
                )
        d = nn(toep[...], jnp.concatenate(pieces, axis=0))
        parts = []
        for h in range(2):
            for j in range(2):
                t = [
                    d[e * 128 + j * 64 : e * 128 + j * 64 + 64, h * 128 : h * 128 + 128] for e in range(3)
                ]
                before = jnp.where(lane == 0, 0.0, pltpu.roll(t[0], 1, 1))
                after = jnp.where(lane == NZ - 1, 0.0, pltpu.roll(t[2], NZ - 1, 1))
                parts.append(before + t[1] + after)
        return parts

    def keep(pair, p, parts):
        c = centre[...]
        parts = [v - c for v in parts]
        sums[...] += (parts[0] + parts[1]) + (parts[2] + parts[3])
        hi, lo = split(jnp.concatenate(parts, axis=1))
        both = jnp.concatenate([hi, lo], axis=0)
        held[pair * 8 + p] = both
        gram[...] += lax.dot_general(both, both, (((1,), (1,)), ((), ())), preferred_element_type=F32)

    gram[...] = jnp.zeros_like(gram)
    sums[...] = jnp.zeros_like(sums)
    first = conv(0, 1)
    total = (first[0] + first[1]) + (first[2] + first[3])
    mean0 = jnp.sum(total, axis=1, keepdims=True) * (1.0 / 512)
    centre[...] = jnp.broadcast_to(mean0, (C, 128))
    keep(0, 1, first)

    def one(pair, p):
        keep(pair, p, conv(pair, p))

    def several(pair, lo, hi):
        for p in range(lo, hi):
            one(pair, p)

    several(0, 2, 4)
    hear(0)
    tell(1)
    several(0, 4, 6)
    hear(1)
    tell(2)
    several(0, 6, 7)

    def clear(cond, x, y, nx, ny):
        @pl.when(cond)
        def _():
            cells[pl.ds(x, nx), pl.ds(y, ny)] = jnp.zeros((nx, ny, C, NZ), BF16)

    x_first, x_last = sx == 0, sx == n_x - 1
    y_first, y_last = sy == 0, sy == n_y - 1
    ycopies[0].wait_recv()
    clear(y_last, 1, BY + 1, BX, 1)
    ycopies[1].wait_recv()
    clear(y_first, 1, 0, BX, 1)
    several(0, 0, 1)
    several(0, 7, 8)

    def corner(f, y, y_edge):
        for d, (x, x_edge) in enumerate(((BX + 1, x_last), (0, x_first))):
            ccopies[2 * d + f].wait_recv()
            clear(jnp.logical_or(x_edge, y_edge), x, y, 1, 1)

    hear(2)
    corner(1, 0, y_first)
    corner(0, BY + 1, y_last)
    for q in range(len(LAST)):
        rows = piece(q)
        xcopies[2 * q].wait_recv()
        clear(x_last, BX + 1, rows.start, 1, rows.size)
        xcopies[2 * q + 1].wait_recv()
        clear(x_first, 0, rows.start, 1, rows.size)
        several(1, LAST[q - 1] if q else 0, LAST[q])

    def turned(col):
        return jnp.sum(eye2 * col, axis=0, keepdims=True)

    H = C // 2
    lane32, row32 = lane[:H], row[:H]
    low = lax.rem(lane32, C)

    def pack(v):
        top = v[:H]
        last = pltpu.roll(v[H:], 128 - H, 1)
        mixed = jnp.where(jnp.logical_and(low < H, row32 > low), last, top)
        diag = jnp.sum(jnp.where(low == row32, last, 0.0), axis=0, keepdims=True)
        return jnp.where(lane32[:16] < C, mixed[:16], mixed[16:]), diag

    dcol = jnp.sum(sums[...], axis=1, keepdims=True) * (1.0 / LOCAL)
    drow = turned(dcol)
    crow = turned(centre[:, 0:1])
    g = gram[:C] + gram[C:]
    g = g + pltpu.roll(g, C, 1)
    products, diag = pack(g - LOCAL * (dcol * drow))
    mean = crow + drow
    lane1 = lane[:1]

    def merge(products, diag, mean, count, n, me, others, moved, s_sem, r_sem):
        high = moved.shape[1] - 16
        rows = row[:high]
        line = jnp.where(lane1 < C, mean, jnp.where(lane1 < C + H, diag, 0.0))
        moved[me, pl.ds(0, 16)] = products
        moved[me, pl.ds(16, high)] = jnp.where(rows == me, line, 0.0)
        copies = [
            send(moved.at[me], moved.at[me], s_sem.at[k], r_sem.at[k], device)
            for k, device in enumerate(others)
        ]
        for cp in copies:
            cp.wait_recv()
        total = moved[0]
        for i in range(1, n):
            total = total + moved[i]
        means = total[16:]
        line = jnp.sum(means, axis=0, keepdims=True)
        mean = jnp.where(lane1 < C, line * (1.0 / n), 0.0)
        off = jnp.where(jnp.logical_and(rows < n, lane[:high] < C), means - mean, 0.0)
        off = off + pltpu.roll(off, C, 1)
        oh, ol = (v.astype(F32) for v in split(off))
        rest = [jnp.zeros((8, 128), F32)] * (high == 8)
        outer = lax.dot_general(
            jnp.concatenate([oh, oh, ol] + rest, axis=0).astype(BF16),
            jnp.concatenate([oh, ol, oh] + rest, axis=0).astype(BF16),
            (((0,), (0,)), ((), ())),
            preferred_element_type=F32,
        )
        more, more_diag = pack(outer[:C])
        return total[:16] + count * more, line + count * more_diag, mean + pltpu.roll(mean, C, 1)

    count = float(LOCAL)
    state = merge(products, diag, mean, count, 2, core, [sibling], moved_c, rc_send, rc_recv)
    count *= 2
    state = merge(
        *state, count, n_chip * n_b, chip * n_b + sb, others_p, moved_p, rp_send, rp_recv
    )
    count *= n_chip * n_b
    products, diag, mean = merge(*state, count, n_x, sx, others_x, moved_x, rx_send, rx_recv)

    half = jnp.concatenate([products, pltpu.roll(products, C, 1)], axis=0)
    across = jnp.concatenate([half, jnp.zeros((128 - H, 128), F32)], axis=0).T
    upper = jnp.where(jnp.logical_and(lane32 < H, row32 > lane32), across[:H], half)
    last = pltpu.roll(jnp.where(row32 > lane32, half, across[:H]), H, 1)
    last = jnp.where(lane32 == row32 + H, pltpu.roll(diag, 128 - H, 1), last)
    lower = jnp.where(lane32 < H, across[H:C], last)
    full = jnp.concatenate([upper, lower], axis=0)[:, :C]
    eye = eye2[:, :C]
    sigma = full * (1.0 / (LOCAL * n_x * n_y * n_b)) + 1e-05 * eye
    trace = jnp.sum(jnp.sum(sigma * eye, axis=1, keepdims=True), axis=0, keepdims=True)
    t = sigma / trace
    f = None
    for turn in range(NS_ITERS):
        step = 1.5 * eye - 0.5 * t
        f = step if f is None else mm(f, step)
        if turn < NS_ITERS - 1:
            t = mm(mm(t, step), step)
    gcp.wait()
    hcp.wait()
    v = vec[...]
    gain_col = jnp.sum(eye * v[0:1], axis=1, keepdims=True)
    shift_col = jnp.sum(eye * v[1:2], axis=1, keepdims=True)
    whiten = f / jnp.sqrt(trace) * gain_col
    bias = shift_col - jnp.sum(whiten * (mean - crow)[:, :C], axis=1, keepdims=True)
    offset[...] = jnp.broadcast_to(bias, (C, 128))
    wh, wl = split(whiten)
    mixer[...] = jnp.concatenate([wh.astype(F32), wh.astype(F32), wl.astype(F32)], axis=1).astype(BF16)
    for cp in sends:
        cp.wait_send()


def mix_body(held, mixer, offset, out, staged, sem):
    bias = offset[...]
    for pair in range(2):
        for p in range(8):
            both = held[pair * 8 + p]
            got = nn(mixer[...], jnp.concatenate([both, both[:C]], axis=0))
            for h in range(2):
                for j in range(2):
                    k = 2 * h + j
                    place = PAIRS[pair][h] * BY + 2 * p + j
                    staged[place] = got[:, k * 128 : k * 128 + 128] + bias
                    pltpu.make_async_copy(staged.at[place], out.at[:, place], sem).start()
    pltpu.make_async_copy(staged, out, sem).wait()


def on_device(volume, conv_weight, out_gain, out_shift):
    n_x, n_y, n_b = (lax.axis_size(a) for a in ("sx", "sy", "batch"))
    weight = jnp.transpose(conv_weight, (2, 3, 4, 0, 1)).reshape(27, C, C)
    anywhere = pl.BlockSpec(memory_space=pl.ANY)
    inside = pl.BlockSpec(memory_space=pltpu.VMEM)
    dma = pltpu.SemaphoreType.DMA
    n_p = n_y // 2 * n_b
    operands = (volume, weight, out_gain.reshape(1, C), out_shift.reshape(1, C))
    held, mixer, offset = pl.pallas_call(
        lambda *refs: body((n_x, n_y, n_b), *refs),
        out_shape=[
            jax.ShapeDtypeStruct((16, 2 * C, 512), BF16),
            jax.ShapeDtypeStruct((C, 3 * C), BF16),
            jax.ShapeDtypeStruct((C, 128), F32),
        ],
        in_specs=[anywhere] * 4,
        out_specs=[inside] * 3,
        scratch_shapes=[
            pltpu.VMEM((BX, C, BY, NZ), BF16),
            pltpu.VMEM((C * BY, NZ), F32),
            pltpu.VMEM((BX + 2, BY + 2, C, NZ), BF16),
            pltpu.VMEM((27, C, C), BF16),
            pltpu.VMEM((384, 768), BF16),
            pltpu.VMEM((2 * C, 2 * C), F32),
            pltpu.VMEM((C, 128), F32),
            pltpu.VMEM((C, 128), F32),
            pltpu.VMEM((2, 24, 128), F32),
            pltpu.VMEM((n_p, 32, 128), F32),
            pltpu.VMEM((n_x, 24, 128), F32),
            pltpu.VMEM((2, C), F32),
            dma((4,)),
            dma,
            dma((2,)),
            dma((2 * len(LAST),)),
            dma((2 * len(LAST),)),
            dma((2,)),
            dma((2,)),
            dma((4,)),
            dma((4,)),
            dma((1,)),
            dma((1,)),
            dma((n_p - 1,)),
            dma((n_p - 1,)),
            dma((n_x - 1,)),
            dma((n_x - 1,)),
            pltpu.SemaphoreType.REGULAR((3, 2)),
        ],
        compiler_params=pltpu.CompilerParams(
            collective_id=0, has_side_effects=True, vmem_limit_bytes=40 * 1024 * 1024
        ),
    )(*(pltpu.with_memory_space_constraint(v, pltpu.HBM) for v in operands))
    result = pl.pallas_call(
        mix_body,
        out_shape=jax.ShapeDtypeStruct((C, BX * BY, NZ), F32),
        in_specs=[inside] * 3,
        out_specs=anywhere,
        scratch_shapes=[pltpu.VMEM((BX * BY, C, NZ), F32), dma],
        compiler_params=pltpu.CompilerParams(vmem_limit_bytes=40 * 1024 * 1024),
    )(held, mixer, offset)
    return result.reshape(1, C, BX, BY, NZ)


def solution(mesh):
    in_specs = (P("batch", None, "sx", "sy", None), P(), P(), P())
    out_specs = P("batch", None, "sx", "sy", None)
    return jax.shard_map(
        on_device, mesh=mesh, in_specs=in_specs, out_specs=out_specs, check_vma=False
    )
```

```python
import jax
import jax.numpy as jnp
from jax import lax
from jax.experimental import pallas as pl
from jax.experimental.pallas import tpu as pltpu
from jax.sharding import PartitionSpec as P

NS_ITERS = 5
C = 64
BX = 4
BY = 16
NZ = 128
LOCAL = BX * BY * NZ
MESH = pl.DeviceIdType.MESH
F32 = jnp.float32
BF16 = jnp.bfloat16
PIECES = ((1, 1), (16, 1), (2, 4), (6, 2), (8, 2), (10, 2), (12, 2), (14, 2))
READY = ((), (), (1,), (2,), (3, 0), (4,), (5,), (6, 7))
PAIRS = ((1, 2), (0, 3))


def split(v):
    hi = v.astype(BF16)
    lo = (v - hi.astype(F32)).astype(BF16)
    return hi, lo


def nn(a, b):
    return lax.dot_general(a, b, (((1,), (0,)), ((), ())), preferred_element_type=F32)


def mm(a, b):
    ah, al = split(a)
    bh, bl = split(b)
    both = nn(jnp.concatenate([ah, al], axis=0), bh)
    return both[:C] + (both[C:] + nn(ah, bl))


def body(
    sizes,
    vol,
    weight,
    gain,
    shift,
    held,
    mixer,
    offset,
    vin,
    wide,
    cells,
    win,
    toep,
    gram,
    sums,
    centre,
    moved_c,
    moved_p,
    moved_x,
    vec,
    load_sem,
    wsem,
    vsem,
    xs_send,
    xs_recv,
    ys_send,
    ys_recv,
    cs_send,
    cs_recv,
    rc_send,
    rc_recv,
    rp_send,
    rp_recv,
    rx_send,
    rx_recv,
    known,
):
    n_x, n_y, n_b = sizes
    sx = lax.axis_index("sx")
    sy = lax.axis_index("sy")
    sb = lax.axis_index("batch")

    def at(n, i, k):
        return lax.rem(i + (k + n), n)

    loads = []
    for k, x in enumerate((0, 3, 1, 2)):
        cp = pltpu.make_async_copy(vol.at[0, :, x], vin.at[x], load_sem.at[k])
        cp.start()
        loads.append(cp)
    wcp = pltpu.make_async_copy(weight, win, wsem)
    wcp.start()
    gcp = pltpu.make_async_copy(gain, vec.at[pl.ds(0, 1)], vsem.at[0])
    gcp.start()
    hcp = pltpu.make_async_copy(shift, vec.at[pl.ds(1, 1)], vsem.at[1])
    hcp.start()

    n_chip = n_y // 2
    core = lax.rem(sy, 2)
    chip = sy // 2
    sibling = {"sy": sy + (1 - 2 * core)}
    others_x = [{"sx": at(n_x, sx, k)} for k in sorted(range(1, n_x), key=lambda k: -min(k, n_x - k))]
    plane = sorted(
        ((j, k) for j in range(n_chip) for k in range(n_b) if j or k),
        key=lambda o: -min(o[0], n_chip - o[0]) - min(o[1], n_b - o[1]),
    )
    others_p = [{"sy": 2 * at(n_chip, chip, j) + core, "batch": at(n_b, sb, k)} for j, k in plane]
    beside = {"sy": at(n_y, sy, 2 * core - 1)}

    barrier = pltpu.get_barrier_semaphore()
    near_x = [{"sx": at(n_x, sx, k)} for k in (-1, 1)]
    near_y = [{"sy": at(n_y, sy, k)} for k in (-2, 2)]
    near_b = [{"batch": at(n_b, sb, k)} for k in (-1, 1)]
    greeted = near_x + [beside, sibling] + near_y + near_b
    for device in greeted:
        pl.semaphore_signal(barrier, inc=1, device_id=device, device_id_type=MESH)

    def tell(k):
        for device in near_x:
            pl.semaphore_signal(known.at[k, 0], inc=1, device_id=device, device_id_type=MESH)
        for device in near_b if k else near_y:
            pl.semaphore_signal(known.at[k, 1], inc=1, device_id=device, device_id_type=MESH)

    def hear(k):
        pl.semaphore_wait(known.at[k, 0], 2)
        pl.semaphore_wait(known.at[k, 1], 2)

    def relay(x):
        wide[...] = vin[x].astype(F32).reshape(C * BY, NZ)
        for y in range(BY):
            cells[x + 1, y + 1] = wide[pl.ds(y, C, stride=BY), :].astype(BF16)

    loads[0].wait()
    relay(0)
    loads[1].wait()
    relay(3)
    pl.semaphore_wait(barrier, len(greeted))

    sends = []

    def send(src, dst, s_sem, r_sem, dev):
        cp = pltpu.make_async_remote_copy(
            src_ref=src, dst_ref=dst, send_sem=s_sem, recv_sem=r_sem, device_id=dev, device_id_type=MESH
        )
        cp.start()
        sends.append(cp)
        return cp

    xcopies = []
    for q, (start, size) in enumerate(PIECES):
        rows = pl.ds(start, size)
        for d, (src_x, dst_x) in enumerate(((1, BX + 1), (BX, 0))):
            xcopies.append(
                send(
                    cells.at[src_x, rows],
                    cells.at[dst_x, rows],
                    xs_send.at[2 * q + d],
                    xs_recv.at[2 * q + d],
                    {"sx": at(n_x, sx, 2 * d - 1)},
                )
            )

    loads[2].wait()
    relay(1)
    loads[3].wait()
    relay(2)
    ycopies = []
    for f, (src_y, dst_y) in enumerate(((1, BY + 1), (BY, 0))):
        ycopies.append(
            send(
                cells.at[pl.ds(1, BX), src_y],
                cells.at[pl.ds(1, BX), dst_y],
                ys_send.at[f],
                ys_recv.at[f],
                {"sy": at(n_y, sy, 2 * f - 1)},
            )
        )

    tell(0)
    wcp.wait()
    zero = jnp.zeros((C, C), F32)
    for a in range(3):
        for e in range(3):
            w = [win[(a * 3 + b) * 3 + e].astype(F32) for b in range(3)]
            blocks = (
                ((w[0], w[1]), (w[2], zero)),
                ((zero, w[0]), (w[1], w[2])),
            )
            for j in range(2):
                for q in range(2):
                    toep[pl.ds(e * 128 + j * 64, 64), pl.ds(a * 256 + q * 128, 128)] = jnp.concatenate(
                        blocks[j][q], axis=1
                    ).astype(BF16)

    lane = lax.broadcasted_iota(jnp.int32, (C, 128), 1)
    row = lax.broadcasted_iota(jnp.int32, (C, 128), 0)
    eye2 = (lax.rem(lane, C) == row).astype(F32)

    def conv(pair, p):
        pieces = []
        for a in range(3):
            for i in range(4):
                pieces.append(
                    jnp.concatenate([cells[x + a, 2 * p + i] for x in PAIRS[pair]], axis=1)
                )
        d = nn(toep[...], jnp.concatenate(pieces, axis=0))
        parts = []
        for h in range(2):
            for j in range(2):
                t = [
                    d[e * 128 + j * 64 : e * 128 + j * 64 + 64, h * 128 : h * 128 + 128] for e in range(3)
                ]
                before = jnp.where(lane == 0, 0.0, pltpu.roll(t[0], 1, 1))
                after = jnp.where(lane == NZ - 1, 0.0, pltpu.roll(t[2], NZ - 1, 1))
                parts.append(before + t[1] + after)
        return parts

    def keep(pair, p, parts):
        c = centre[...]
        parts = [v - c for v in parts]
        sums[...] += (parts[0] + parts[1]) + (parts[2] + parts[3])
        hi, lo = split(jnp.concatenate(parts, axis=1))
        both = jnp.concatenate([hi, lo], axis=0)
        held[pair * 8 + p] = both
        gram[...] += lax.dot_general(both, both, (((1,), (1,)), ((), ())), preferred_element_type=F32)

    gram[...] = jnp.zeros_like(gram)
    sums[...] = jnp.zeros_like(sums)
    first = conv(0, 1)
    total = (first[0] + first[1]) + (first[2] + first[3])
    mean0 = jnp.sum(total, axis=1, keepdims=True) * (1.0 / 512)
    centre[...] = jnp.broadcast_to(mean0, (C, 128))
    keep(0, 1, first)

    def one(pair, p):
        keep(pair, p, conv(pair, p))

    def several(pair, lo, hi):
        for p in range(lo, hi):
            one(pair, p)

    several(0, 2, 4)
    hear(0)
    tell(1)
    several(0, 4, 6)
    hear(1)
    tell(2)
    several(0, 6, 7)

    def clear(cond, x, y, nx, ny):
        @pl.when(cond)
        def _():
            cells[pl.ds(x, nx), pl.ds(y, ny)] = jnp.zeros((nx, ny, C, NZ), BF16)

    x_first, x_last = sx == 0, sx == n_x - 1
    y_first, y_last = sy == 0, sy == n_y - 1
    def arrive(q):
        start, size = PIECES[q]
        xcopies[2 * q].wait_recv()
        clear(x_last, BX + 1, start, 1, size)
        xcopies[2 * q + 1].wait_recv()
        clear(x_first, 0, start, 1, size)

    arrive(0)
    arrive(1)
    ccopies = []
    for d, x in enumerate((BX + 1, 0)):
        for f, (src_y, dst_y) in enumerate(((1, BY + 1), (BY, 0))):
            ccopies.append(
                send(
                    cells.at[x, src_y],
                    cells.at[x, dst_y],
                    cs_send.at[2 * d + f],
                    cs_recv.at[2 * d + f],
                    {"sy": at(n_y, sy, 2 * f - 1)},
                )
            )


    ycopies[0].wait_recv()
    clear(y_last, 1, BY + 1, BX, 1)
    ycopies[1].wait_recv()
    clear(y_first, 1, 0, BX, 1)
    several(0, 0, 1)
    several(0, 7, 8)

    def corner(f, y, y_edge):
        for d, (x, x_edge) in enumerate(((BX + 1, x_last), (0, x_first))):
            ccopies[2 * d + f].wait_recv()
            clear(jnp.logical_or(x_edge, y_edge), x, y, 1, 1)

    hear(2)
    for q in range(2, len(PIECES)):
        arrive(q)
        for p in READY[q]:
            if p == 0:
                corner(1, 0, y_first)
            elif p == 7:
                corner(0, BY + 1, y_last)
            one(1, p)

    def turned(col):
        return jnp.sum(eye2 * col, axis=0, keepdims=True)

    H = C // 2
    lane32, row32 = lane[:H], row[:H]
    low = lax.rem(lane32, C)

    def pack(v):
        top = v[:H]
        last = pltpu.roll(v[H:], 128 - H, 1)
        mixed = jnp.where(jnp.logical_and(low < H, row32 > low), last, top)
        diag = jnp.sum(jnp.where(low == row32, last, 0.0), axis=0, keepdims=True)
        return jnp.where(lane32[:16] < C, mixed[:16], mixed[16:]), diag

    dcol = jnp.sum(sums[...], axis=1, keepdims=True) * (1.0 / LOCAL)
    drow = turned(dcol)
    crow = turned(centre[:, 0:1])
    g = gram[:C] + gram[C:]
    g = g + pltpu.roll(g, C, 1)
    products, diag = pack(g - LOCAL * (dcol * drow))
    mean = crow + drow
    lane1 = lane[:1]

    def merge(products, diag, mean, count, n, me, others, moved, s_sem, r_sem):
        high = moved.shape[1] - 16
        rows = row[:high]
        line = jnp.where(lane1 < C, mean, jnp.where(lane1 < C + H, diag, 0.0))
        moved[me, pl.ds(0, 16)] = products
        moved[me, pl.ds(16, high)] = jnp.where(rows == me, line, 0.0)
        copies = [
            send(moved.at[me], moved.at[me], s_sem.at[k], r_sem.at[k], device)
            for k, device in enumerate(others)
        ]
        for cp in copies:
            cp.wait_recv()
        parts = [moved[i] for i in range(n)]
        while len(parts) > 1:
            parts = [u + v for u, v in zip(parts[::2], parts[1::2])]
        total = parts[0]
        means = total[16:]
        line = jnp.sum(means, axis=0, keepdims=True)
        mean = jnp.where(lane1 < C, line * (1.0 / n), 0.0)
        off = jnp.where(jnp.logical_and(rows < n, lane[:high] < C), means - mean, 0.0)
        off = off + pltpu.roll(off, C, 1)
        oh, ol = (v.astype(F32) for v in split(off))
        rest = [jnp.zeros((8, 128), F32)] * (high == 8)
        outer = lax.dot_general(
            jnp.concatenate([oh, oh, ol] + rest, axis=0).astype(BF16),
            jnp.concatenate([oh, ol, oh] + rest, axis=0).astype(BF16),
            (((0,), (0,)), ((), ())),
            preferred_element_type=F32,
        )
        more, more_diag = pack(outer[:C])
        return total[:16] + count * more, line + count * more_diag, mean + pltpu.roll(mean, C, 1)

    count = float(LOCAL)
    state = merge(products, diag, mean, count, 2, core, [sibling], moved_c, rc_send, rc_recv)
    count *= 2
    state = merge(*state, count, n_x, sx, others_x, moved_x, rx_send, rx_recv)
    count *= n_x
    products, diag, mean = merge(
        *state, count, n_chip * n_b, chip * n_b + sb, others_p, moved_p, rp_send, rp_recv
    )

    half = jnp.concatenate([products, pltpu.roll(products, C, 1)], axis=0)
    across = jnp.concatenate([half, jnp.zeros((128 - H, 128), F32)], axis=0).T
    upper = jnp.where(jnp.logical_and(lane32 < H, row32 > lane32), across[:H], half)
    last = pltpu.roll(jnp.where(row32 > lane32, half, across[:H]), H, 1)
    last = jnp.where(lane32 == row32 + H, pltpu.roll(diag, 128 - H, 1), last)
    lower = jnp.where(lane32 < H, across[H:C], last)
    full = jnp.concatenate([upper, lower], axis=0)[:, :C]
    eye = eye2[:, :C]
    sigma = full * (1.0 / (LOCAL * n_x * n_y * n_b)) + 1e-05 * eye
    trace = jnp.sum(jnp.sum(sigma * eye, axis=1, keepdims=True), axis=0, keepdims=True)
    t = sigma / trace
    f = None
    for turn in range(NS_ITERS):
        step = 1.5 * eye - 0.5 * t
        f = step if f is None else mm(f, step)
        if turn < NS_ITERS - 1:
            t = mm(mm(t, step), step)
    gcp.wait()
    hcp.wait()
    v = vec[...]
    gain_col = jnp.sum(eye * v[0:1], axis=1, keepdims=True)
    shift_col = jnp.sum(eye * v[1:2], axis=1, keepdims=True)
    whiten = f / jnp.sqrt(trace) * gain_col
    bias = shift_col - jnp.sum(whiten * (mean - crow)[:, :C], axis=1, keepdims=True)
    offset[...] = jnp.broadcast_to(bias, (C, 128))
    wh, wl = split(whiten)
    mixer[...] = jnp.concatenate([wh.astype(F32), wh.astype(F32), wl.astype(F32)], axis=1).astype(BF16)
    for cp in sends:
        cp.wait_send()


def mix_body(held, mixer, offset, out, staged, sem):
    bias = offset[...]
    for pair in range(2):
        for p in range(8):
            both = held[pair * 8 + p]
            got = nn(mixer[...], jnp.concatenate([both, both[:C]], axis=0))
            for h in range(2):
                for j in range(2):
                    k = 2 * h + j
                    place = PAIRS[pair][h] * BY + 2 * p + j
                    staged[place] = got[:, k * 128 : k * 128 + 128] + bias
                    pltpu.make_async_copy(staged.at[place], out.at[:, place], sem).start()
    pltpu.make_async_copy(staged, out, sem).wait()


def on_device(volume, conv_weight, out_gain, out_shift):
    n_x, n_y, n_b = (lax.axis_size(a) for a in ("sx", "sy", "batch"))
    weight = jnp.transpose(conv_weight, (2, 3, 4, 0, 1)).reshape(27, C, C)
    anywhere = pl.BlockSpec(memory_space=pl.ANY)
    inside = pl.BlockSpec(memory_space=pltpu.VMEM)
    dma = pltpu.SemaphoreType.DMA
    n_p = n_y // 2 * n_b
    operands = (volume, weight, out_gain.reshape(1, C), out_shift.reshape(1, C))
    held, mixer, offset = pl.pallas_call(
        lambda *refs: body((n_x, n_y, n_b), *refs),
        out_shape=[
            jax.ShapeDtypeStruct((16, 2 * C, 512), BF16),
            jax.ShapeDtypeStruct((C, 3 * C), BF16),
            jax.ShapeDtypeStruct((C, 128), F32),
        ],
        in_specs=[anywhere] * 4,
        out_specs=[inside] * 3,
        scratch_shapes=[
            pltpu.VMEM((BX, C, BY, NZ), BF16),
            pltpu.VMEM((C * BY, NZ), F32),
            pltpu.VMEM((BX + 2, BY + 2, C, NZ), BF16),
            pltpu.VMEM((27, C, C), BF16),
            pltpu.VMEM((384, 768), BF16),
            pltpu.VMEM((2 * C, 2 * C), F32),
            pltpu.VMEM((C, 128), F32),
            pltpu.VMEM((C, 128), F32),
            pltpu.VMEM((2, 24, 128), F32),
            pltpu.VMEM((n_p, 32, 128), F32),
            pltpu.VMEM((n_x, 24, 128), F32),
            pltpu.VMEM((2, C), F32),
            dma((4,)),
            dma,
            dma((2,)),
            dma((2 * len(PIECES),)),
            dma((2 * len(PIECES),)),
            dma((2,)),
            dma((2,)),
            dma((4,)),
            dma((4,)),
            dma((1,)),
            dma((1,)),
            dma((n_p - 1,)),
            dma((n_p - 1,)),
            dma((n_x - 1,)),
            dma((n_x - 1,)),
            pltpu.SemaphoreType.REGULAR((3, 2)),
        ],
        compiler_params=pltpu.CompilerParams(
            collective_id=0, has_side_effects=True, vmem_limit_bytes=40 * 1024 * 1024
        ),
    )(*(pltpu.with_memory_space_constraint(v, pltpu.HBM) for v in operands))
    result = pl.pallas_call(
        mix_body,
        out_shape=jax.ShapeDtypeStruct((C, BX * BY, NZ), F32),
        in_specs=[inside] * 3,
        out_specs=anywhere,
        scratch_shapes=[pltpu.VMEM((BX * BY, C, NZ), F32), dma],
        compiler_params=pltpu.CompilerParams(vmem_limit_bytes=40 * 1024 * 1024),
    )(held, mixer, offset)
    return result.reshape(1, C, BX, BY, NZ)


def solution(mesh):
    in_specs = (P("batch", None, "sx", "sy", None), P(), P(), P())
    out_specs = P("batch", None, "sx", "sy", None)
    return jax.shard_map(
        on_device, mesh=mesh, in_specs=in_specs, out_specs=out_specs, check_vma=False
    )
```

```python
import jax
import jax.numpy as jnp
from jax import lax
from jax.experimental import pallas as pl
from jax.experimental.pallas import tpu as pltpu
from jax.sharding import PartitionSpec as P

NS_ITERS = 5
C = 64
BX = 4
BY = 16
NZ = 128
LOCAL = BX * BY * NZ
MESH = pl.DeviceIdType.MESH
F32 = jnp.float32
BF16 = jnp.bfloat16
PIECES = ((1, 1), (16, 1), (2, 4), (6, 2), (8, 2), (10, 2), (12, 2), (14, 2))
READY = ((), (), (1,), (2,), (3, 0), (4,), (5,), (6, 7))
PAIRS = ((1, 2), (0, 3))


def split(v):
    hi = v.astype(BF16)
    lo = (v - hi.astype(F32)).astype(BF16)
    return hi, lo


def nn(a, b):
    return lax.dot_general(a, b, (((1,), (0,)), ((), ())), preferred_element_type=F32)


def mm(a, b):
    ah, al = split(a)
    bh, bl = split(b)
    both = nn(jnp.concatenate([ah, al], axis=0), bh)
    return both[:C] + (both[C:] + nn(ah, bl))


def body(
    sizes,
    vol,
    weight,
    gain,
    shift,
    held,
    mixer,
    offset,
    vin,
    wide,
    cells,
    win,
    toep,
    gram,
    sums,
    centre,
    moved_c,
    moved_p,
    moved_x,
    vec,
    load_sem,
    wsem,
    vsem,
    xs_send,
    xs_recv,
    ys_send,
    ys_recv,
    cs_send,
    cs_recv,
    rc_send,
    rc_recv,
    rp_send,
    rp_recv,
    rx_send,
    rx_recv,
    known,
):
    n_x, n_y, n_b = sizes
    sx = lax.axis_index("sx")
    sy = lax.axis_index("sy")
    sb = lax.axis_index("batch")

    def at(n, i, k):
        return lax.rem(i + (k + n), n)

    loads = []
    for k, x in enumerate((0, 3, 1, 2)):
        cp = pltpu.make_async_copy(vol.at[0, :, x], vin.at[x], load_sem.at[k])
        cp.start()
        loads.append(cp)
    wcp = pltpu.make_async_copy(weight, win, wsem)
    wcp.start()
    gcp = pltpu.make_async_copy(gain, vec.at[pl.ds(0, 1)], vsem.at[0])
    gcp.start()
    hcp = pltpu.make_async_copy(shift, vec.at[pl.ds(1, 1)], vsem.at[1])
    hcp.start()

    n_chip = n_y // 2
    core = lax.rem(sy, 2)
    chip = sy // 2
    sibling = {"sy": sy + (1 - 2 * core)}
    others_x = [{"sx": at(n_x, sx, k)} for k in sorted(range(1, n_x), key=lambda k: -min(k, n_x - k))]
    plane = sorted(
        ((j, k) for j in range(n_chip) for k in range(n_b) if j or k),
        key=lambda o: -min(o[0], n_chip - o[0]) - min(o[1], n_b - o[1]),
    )
    others_p = [{"sy": 2 * at(n_chip, chip, j) + core, "batch": at(n_b, sb, k)} for j, k in plane]
    beside = {"sy": at(n_y, sy, 2 * core - 1)}

    barrier = pltpu.get_barrier_semaphore()
    near_x = [{"sx": at(n_x, sx, k)} for k in (-1, 1)]
    near_y = [{"sy": at(n_y, sy, k)} for k in (-2, 2)]
    near_b = [{"batch": at(n_b, sb, k)} for k in (-1, 1)]
    greeted = near_x + [beside, sibling] + near_y + near_b
    for device in greeted:
        pl.semaphore_signal(barrier, inc=1, device_id=device, device_id_type=MESH)

    def tell(k):
        for device in near_x:
            pl.semaphore_signal(known.at[k, 0], inc=1, device_id=device, device_id_type=MESH)
        for device in near_b if k else near_y:
            pl.semaphore_signal(known.at[k, 1], inc=1, device_id=device, device_id_type=MESH)

    def hear(k):
        pl.semaphore_wait(known.at[k, 0], 2)
        pl.semaphore_wait(known.at[k, 1], 2)

    def relay(x):
        wide[...] = vin[x].astype(F32).reshape(C * BY, NZ)
        for y in range(BY):
            cells[x + 1, y + 1] = wide[pl.ds(y, C, stride=BY), :].astype(BF16)

    loads[0].wait()
    relay(0)
    loads[1].wait()
    relay(3)
    pl.semaphore_wait(barrier, len(greeted))

    sends = []

    def send(src, dst, s_sem, r_sem, dev):
        cp = pltpu.make_async_remote_copy(
            src_ref=src, dst_ref=dst, send_sem=s_sem, recv_sem=r_sem, device_id=dev, device_id_type=MESH
        )
        cp.start()
        sends.append(cp)
        return cp

    xcopies = []
    for q, (start, size) in enumerate(PIECES):
        rows = pl.ds(start, size)
        for d, (src_x, dst_x) in enumerate(((1, BX + 1), (BX, 0))):
            xcopies.append(
                send(
                    cells.at[src_x, rows],
                    cells.at[dst_x, rows],
                    xs_send.at[2 * q + d],
                    xs_recv.at[2 * q + d],
                    {"sx": at(n_x, sx, 2 * d - 1)},
                )
            )

    loads[2].wait()
    relay(1)
    loads[3].wait()
    relay(2)
    ycopies = []
    for f, (src_y, dst_y) in enumerate(((1, BY + 1), (BY, 0))):
        ycopies.append(
            send(
                cells.at[pl.ds(1, BX), src_y],
                cells.at[pl.ds(1, BX), dst_y],
                ys_send.at[f],
                ys_recv.at[f],
                {"sy": at(n_y, sy, 2 * f - 1)},
            )
        )

    tell(0)
    wcp.wait()
    zero = jnp.zeros((C, C), F32)
    for a in range(3):
        for e in range(3):
            w = [win[(a * 3 + b) * 3 + e].astype(F32) for b in range(3)]
            blocks = (
                ((w[0], w[1]), (w[2], zero)),
                ((zero, w[0]), (w[1], w[2])),
            )
            for j in range(2):
                for q in range(2):
                    toep[pl.ds(e * 128 + j * 64, 64), pl.ds(a * 256 + q * 128, 128)] = jnp.concatenate(
                        blocks[j][q], axis=1
                    ).astype(BF16)

    lane = lax.broadcasted_iota(jnp.int32, (C, 128), 1)
    row = lax.broadcasted_iota(jnp.int32, (C, 128), 0)
    eye2 = (lax.rem(lane, C) == row).astype(F32)

    def conv(pair, p):
        pieces = []
        for a in range(3):
            for i in range(4):
                pieces.append(
                    jnp.concatenate([cells[x + a, 2 * p + i] for x in PAIRS[pair]], axis=1)
                )
        d = nn(toep[...], jnp.concatenate(pieces, axis=0))
        parts = []
        for h in range(2):
            for j in range(2):
                t = [
                    d[e * 128 + j * 64 : e * 128 + j * 64 + 64, h * 128 : h * 128 + 128] for e in range(3)
                ]
                before = jnp.where(lane == 0, 0.0, pltpu.roll(t[0], 1, 1))
                after = jnp.where(lane == NZ - 1, 0.0, pltpu.roll(t[2], NZ - 1, 1))
                parts.append(before + t[1] + after)
        return parts

    def keep(pair, p, parts):
        c = centre[...]
        parts = [v - c for v in parts]
        sums[...] += (parts[0] + parts[1]) + (parts[2] + parts[3])
        hi, lo = split(jnp.concatenate(parts, axis=1))
        both = jnp.concatenate([hi, lo], axis=0)
        held[pair * 8 + p] = both
        gram[...] += lax.dot_general(both, both, (((1,), (1,)), ((), ())), preferred_element_type=F32)

    gram[...] = jnp.zeros_like(gram)
    sums[...] = jnp.zeros_like(sums)
    first = conv(0, 1)
    total = (first[0] + first[1]) + (first[2] + first[3])
    mean0 = jnp.sum(total, axis=1, keepdims=True) * (1.0 / 512)
    centre[...] = jnp.broadcast_to(mean0, (C, 128))
    keep(0, 1, first)

    def one(pair, p):
        keep(pair, p, conv(pair, p))

    def several(pair, lo, hi):
        for p in range(lo, hi):
            one(pair, p)

    several(0, 2, 4)
    hear(0)
    tell(1)
    several(0, 4, 6)
    hear(1)
    tell(2)
    several(0, 6, 7)

    def clear(cond, x, y, nx, ny):
        @pl.when(cond)
        def _():
            cells[pl.ds(x, nx), pl.ds(y, ny)] = jnp.zeros((nx, ny, C, NZ), BF16)

    x_first, x_last = sx == 0, sx == n_x - 1
    y_first, y_last = sy == 0, sy == n_y - 1
    def arrive(q):
        start, size = PIECES[q]
        xcopies[2 * q].wait_recv()
        clear(x_last, BX + 1, start, 1, size)
        xcopies[2 * q + 1].wait_recv()
        clear(x_first, 0, start, 1, size)

    arrive(0)
    arrive(1)
    ccopies = []
    for d, x in enumerate((BX + 1, 0)):
        for f, (src_y, dst_y) in enumerate(((1, BY + 1), (BY, 0))):
            ccopies.append(
                send(
                    cells.at[x, src_y],
                    cells.at[x, dst_y],
                    cs_send.at[2 * d + f],
                    cs_recv.at[2 * d + f],
                    {"sy": at(n_y, sy, 2 * f - 1)},
                )
            )


    ycopies[0].wait_recv()
    clear(y_last, 1, BY + 1, BX, 1)
    ycopies[1].wait_recv()
    clear(y_first, 1, 0, BX, 1)
    several(0, 0, 1)
    several(0, 7, 8)

    def corner(f, y, y_edge):
        for d, (x, x_edge) in enumerate(((BX + 1, x_last), (0, x_first))):
            ccopies[2 * d + f].wait_recv()
            clear(jnp.logical_or(x_edge, y_edge), x, y, 1, 1)

    hear(2)
    for q in range(2, len(PIECES)):
        arrive(q)
        for p in READY[q]:
            if p == 0:
                corner(1, 0, y_first)
            elif p == 7:
                corner(0, BY + 1, y_last)
            one(1, p)

    def turned(col):
        return jnp.sum(eye2 * col, axis=0, keepdims=True)

    H = C // 2
    lane32, row32 = lane[:H], row[:H]
    low = lax.rem(lane32, C)

    def pack(v):
        top = v[:H]
        last = pltpu.roll(v[H:], 128 - H, 1)
        mixed = jnp.where(jnp.logical_and(low < H, row32 > low), last, top)
        diag = jnp.sum(jnp.where(low == row32, last, 0.0), axis=0, keepdims=True)
        return jnp.where(lane32[:16] < C, mixed[:16], mixed[16:]), diag

    dcol = jnp.sum(sums[...], axis=1, keepdims=True) * (1.0 / LOCAL)
    drow = turned(dcol)
    crow = turned(centre[:, 0:1])
    g = gram[:C] + gram[C:]
    g = g + pltpu.roll(g, C, 1)
    products, diag = pack(g - LOCAL * (dcol * drow))
    mean = crow + drow
    lane1 = lane[:1]

    def merge(products, diag, mean, count, n, me, others, moved, s_sem, r_sem):
        high = 8 if n <= 8 else 16
        rows = row[:high]
        line = jnp.where(lane1 < C, mean, jnp.where(lane1 < C + H, diag, 0.0))
        moved[me, pl.ds(0, 16)] = products
        moved[me, pl.ds(16, 1)] = line
        used = moved.at[me, pl.ds(0, 17)]
        copies = [
            send(used, used, s_sem.at[k], r_sem.at[k], device)
            for k, device in enumerate(others)
        ]
        for cp in copies:
            cp.wait_recv()
        def tree(parts):
            while len(parts) > 1:
                parts = [u + v for u, v in zip(parts[::2], parts[1::2])]
            return parts[0]

        total = tree([moved[i, pl.ds(0, 16)] for i in range(n)])
        means = tree([jnp.where(rows == i, moved[i, pl.ds(16, 1)], 0.0) for i in range(n)])
        line = jnp.sum(means, axis=0, keepdims=True)
        mean = jnp.where(lane1 < C, line * (1.0 / n), 0.0)
        off = jnp.where(jnp.logical_and(rows < n, lane[:high] < C), means - mean, 0.0)
        off = off + pltpu.roll(off, C, 1)
        oh, ol = (v.astype(F32) for v in split(off))
        rest = [jnp.zeros((8, 128), F32)] * (high == 8)
        outer = lax.dot_general(
            jnp.concatenate([oh, oh, ol] + rest, axis=0).astype(BF16),
            jnp.concatenate([oh, ol, oh] + rest, axis=0).astype(BF16),
            (((0,), (0,)), ((), ())),
            preferred_element_type=F32,
        )
        more, more_diag = pack(outer[:C])
        return total + count * more, line + count * more_diag, mean + pltpu.roll(mean, C, 1)

    count = float(LOCAL)
    state = merge(products, diag, mean, count, 2, core, [sibling], moved_c, rc_send, rc_recv)
    count *= 2
    state = merge(*state, count, n_x, sx, others_x, moved_x, rx_send, rx_recv)
    count *= n_x
    products, diag, mean = merge(
        *state, count, n_chip * n_b, chip * n_b + sb, others_p, moved_p, rp_send, rp_recv
    )

    half = jnp.concatenate([products, pltpu.roll(products, C, 1)], axis=0)
    across = jnp.concatenate([half, jnp.zeros((128 - H, 128), F32)], axis=0).T
    upper = jnp.where(jnp.logical_and(lane32 < H, row32 > lane32), across[:H], half)
    last = pltpu.roll(jnp.where(row32 > lane32, half, across[:H]), H, 1)
    last = jnp.where(lane32 == row32 + H, pltpu.roll(diag, 128 - H, 1), last)
    lower = jnp.where(lane32 < H, across[H:C], last)
    full = jnp.concatenate([upper, lower], axis=0)[:, :C]
    eye = eye2[:, :C]
    sigma = full * (1.0 / (LOCAL * n_x * n_y * n_b)) + 1e-05 * eye
    trace = jnp.sum(jnp.sum(sigma * eye, axis=1, keepdims=True), axis=0, keepdims=True)
    t = sigma / trace
    f = None
    for turn in range(NS_ITERS):
        step = 1.5 * eye - 0.5 * t
        f = step if f is None else mm(f, step)
        if turn < NS_ITERS - 1:
            t = mm(mm(t, step), step)
    gcp.wait()
    hcp.wait()
    v = vec[...]
    gain_col = jnp.sum(eye * v[0:1], axis=1, keepdims=True)
    shift_col = jnp.sum(eye * v[1:2], axis=1, keepdims=True)
    whiten = f / jnp.sqrt(trace) * gain_col
    bias = shift_col - jnp.sum(whiten * (mean - crow)[:, :C], axis=1, keepdims=True)
    offset[...] = jnp.broadcast_to(bias, (C, 128))
    wh, wl = split(whiten)
    mixer[...] = jnp.concatenate([wh.astype(F32), wh.astype(F32), wl.astype(F32)], axis=1).astype(BF16)
    for cp in sends:
        cp.wait_send()


def mix_body(held, mixer, offset, out, staged, sem):
    bias = offset[...]
    for pair in range(2):
        for p in range(8):
            both = held[pair * 8 + p]
            got = nn(mixer[...], jnp.concatenate([both, both[:C]], axis=0))
            for h in range(2):
                for j in range(2):
                    k = 2 * h + j
                    place = PAIRS[pair][h] * BY + 2 * p + j
                    staged[place] = got[:, k * 128 : k * 128 + 128] + bias
                    pltpu.make_async_copy(staged.at[place], out.at[:, place], sem).start()
    pltpu.make_async_copy(staged, out, sem).wait()


def on_device(volume, conv_weight, out_gain, out_shift):
    n_x, n_y, n_b = (lax.axis_size(a) for a in ("sx", "sy", "batch"))
    weight = jnp.transpose(conv_weight, (2, 3, 4, 0, 1)).reshape(27, C, C)
    anywhere = pl.BlockSpec(memory_space=pl.ANY)
    inside = pl.BlockSpec(memory_space=pltpu.VMEM)
    dma = pltpu.SemaphoreType.DMA
    n_p = n_y // 2 * n_b
    operands = (volume, weight, out_gain.reshape(1, C), out_shift.reshape(1, C))
    held, mixer, offset = pl.pallas_call(
        lambda *refs: body((n_x, n_y, n_b), *refs),
        out_shape=[
            jax.ShapeDtypeStruct((16, 2 * C, 512), BF16),
            jax.ShapeDtypeStruct((C, 3 * C), BF16),
            jax.ShapeDtypeStruct((C, 128), F32),
        ],
        in_specs=[anywhere] * 4,
        out_specs=[inside] * 3,
        scratch_shapes=[
            pltpu.VMEM((BX, C, BY, NZ), BF16),
            pltpu.VMEM((C * BY, NZ), F32),
            pltpu.VMEM((BX + 2, BY + 2, C, NZ), BF16),
            pltpu.VMEM((27, C, C), BF16),
            pltpu.VMEM((384, 768), BF16),
            pltpu.VMEM((2 * C, 2 * C), F32),
            pltpu.VMEM((C, 128), F32),
            pltpu.VMEM((C, 128), F32),
            pltpu.VMEM((2, 24, 128), F32),
            pltpu.VMEM((n_p, 24, 128), F32),
            pltpu.VMEM((n_x, 24, 128), F32),
            pltpu.VMEM((2, C), F32),
            dma((4,)),
            dma,
            dma((2,)),
            dma((2 * len(PIECES),)),
            dma((2 * len(PIECES),)),
            dma((2,)),
            dma((2,)),
            dma((4,)),
            dma((4,)),
            dma((1,)),
            dma((1,)),
            dma((n_p - 1,)),
            dma((n_p - 1,)),
            dma((n_x - 1,)),
            dma((n_x - 1,)),
            pltpu.SemaphoreType.REGULAR((3, 2)),
        ],
        compiler_params=pltpu.CompilerParams(
            collective_id=0, has_side_effects=True, vmem_limit_bytes=40 * 1024 * 1024
        ),
    )(*(pltpu.with_memory_space_constraint(v, pltpu.HBM) for v in operands))
    result = pl.pallas_call(
        mix_body,
        out_shape=jax.ShapeDtypeStruct((C, BX * BY, NZ), F32),
        in_specs=[inside] * 3,
        out_specs=anywhere,
        scratch_shapes=[pltpu.VMEM((BX * BY, C, NZ), F32), dma],
        compiler_params=pltpu.CompilerParams(vmem_limit_bytes=40 * 1024 * 1024),
    )(held, mixer, offset)
    return result.reshape(1, C, BX, BY, NZ)


def solution(mesh):
    in_specs = (P("batch", None, "sx", "sy", None), P(), P(), P())
    out_specs = P("batch", None, "sx", "sy", None)
    return jax.shard_map(
        on_device, mesh=mesh, in_specs=in_specs, out_specs=out_specs, check_vma=False
    )
```

```python
import jax
import jax.numpy as jnp
from jax import lax
from jax.experimental import pallas as pl
from jax.experimental.pallas import tpu as pltpu
from jax.sharding import PartitionSpec as P

NS_ITERS = 5
C = 64
BX = 4
BY = 16
NZ = 128
LOCAL = BX * BY * NZ
MESH = pl.DeviceIdType.MESH
F32 = jnp.float32
BF16 = jnp.bfloat16
PIECES = ((1, 1), (16, 1), (2, 4), (6, 2), (8, 2), (10, 2), (12, 2), (14, 2))
READY = ((), (), (1,), (2,), (3, 0), (4,), (5,), (6, 7))
PAIRS = ((1, 2), (0, 3))


def split(v):
    hi = v.astype(BF16)
    lo = (v - hi.astype(F32)).astype(BF16)
    return hi, lo


def nn(a, b):
    return lax.dot_general(a, b, (((1,), (0,)), ((), ())), preferred_element_type=F32)


def mm(a, b):
    ah, al = split(a)
    bh, bl = split(b)
    both = nn(jnp.concatenate([ah, al], axis=0), bh)
    return both[:C] + (both[C:] + nn(ah, bl))


def body(
    sizes,
    vol,
    weight,
    gain,
    shift,
    held,
    mixer,
    offset,
    vin,
    wide,
    cells,
    win,
    toep,
    gram,
    sums,
    centre,
    moved_c,
    moved_p,
    moved_x,
    vec,
    load_sem,
    wsem,
    vsem,
    xs_send,
    xs_recv,
    ys_send,
    ys_recv,
    cs_send,
    cs_recv,
    rc_send,
    rc_recv,
    rp_send,
    rp_recv,
    rx_send,
    rx_recv,
    known,
):
    n_x, n_y, n_b = sizes
    sx = lax.axis_index("sx")
    sy = lax.axis_index("sy")
    sb = lax.axis_index("batch")

    def at(n, i, k):
        return lax.rem(i + (k + n), n)

    n_chip = n_y // 2
    core = lax.rem(sy, 2)
    chip = sy // 2
    sibling = {"sy": sy + (1 - 2 * core)}
    others_x = [{"sx": at(n_x, sx, k)} for k in sorted(range(1, n_x), key=lambda k: -min(k, n_x - k))]
    plane = sorted(
        ((j, k) for j in range(n_chip) for k in range(n_b) if j or k),
        key=lambda o: -min(o[0], n_chip - o[0]) - min(o[1], n_b - o[1]),
    )
    others_p = [{"sy": 2 * at(n_chip, chip, j) + core, "batch": at(n_b, sb, k)} for j, k in plane]
    beside = {"sy": at(n_y, sy, 2 * core - 1)}

    barrier = pltpu.get_barrier_semaphore()
    near_x = [{"sx": at(n_x, sx, k)} for k in (-1, 1)]
    near_y = [{"sy": at(n_y, sy, k)} for k in (-2, 2)]
    near_b = [{"batch": at(n_b, sb, k)} for k in (-1, 1)]
    greeted = near_x + [beside, sibling] + near_y + near_b
    for device in greeted:
        pl.semaphore_signal(barrier, inc=1, device_id=device, device_id_type=MESH)

    loads = []
    for k, x in enumerate((0, 3, 1, 2)):
        cp = pltpu.make_async_copy(vol.at[0, :, x], vin.at[x], load_sem.at[k])
        cp.start()
        loads.append(cp)
    wcp = pltpu.make_async_copy(weight, win, wsem)
    wcp.start()
    gcp = pltpu.make_async_copy(gain, vec.at[pl.ds(0, 1)], vsem.at[0])
    gcp.start()
    hcp = pltpu.make_async_copy(shift, vec.at[pl.ds(1, 1)], vsem.at[1])
    hcp.start()

    def tell(k):
        for device in near_x:
            pl.semaphore_signal(known.at[k, 0], inc=1, device_id=device, device_id_type=MESH)
        for device in near_b if k else near_y:
            pl.semaphore_signal(known.at[k, 1], inc=1, device_id=device, device_id_type=MESH)

    def hear(k):
        pl.semaphore_wait(known.at[k, 0], 2)
        pl.semaphore_wait(known.at[k, 1], 2)

    def relay(x):
        wide[...] = vin[x].astype(F32).reshape(C * BY, NZ)
        for y in range(BY):
            cells[x + 1, y + 1] = wide[pl.ds(y, C, stride=BY), :].astype(BF16)

    loads[0].wait()
    relay(0)
    loads[1].wait()
    relay(3)
    pl.semaphore_wait(barrier, len(greeted))

    sends = []

    def send(src, dst, s_sem, r_sem, dev):
        cp = pltpu.make_async_remote_copy(
            src_ref=src, dst_ref=dst, send_sem=s_sem, recv_sem=r_sem, device_id=dev, device_id_type=MESH
        )
        cp.start()
        sends.append(cp)
        return cp

    xcopies = []
    for q, (start, size) in enumerate(PIECES):
        rows = pl.ds(start, size)
        for d, (src_x, dst_x) in enumerate(((1, BX + 1), (BX, 0))):
            xcopies.append(
                send(
                    cells.at[src_x, rows],
                    cells.at[dst_x, rows],
                    xs_send.at[2 * q + d],
                    xs_recv.at[2 * q + d],
                    {"sx": at(n_x, sx, 2 * d - 1)},
                )
            )

    loads[2].wait()
    relay(1)
    loads[3].wait()
    relay(2)
    ycopies = []
    for f, (src_y, dst_y) in enumerate(((1, BY + 1), (BY, 0))):
        ycopies.append(
            send(
                cells.at[pl.ds(1, BX), src_y],
                cells.at[pl.ds(1, BX), dst_y],
                ys_send.at[f],
                ys_recv.at[f],
                {"sy": at(n_y, sy, 2 * f - 1)},
            )
        )

    tell(0)
    wcp.wait()
    zero = jnp.zeros((C, C), F32)
    for a in range(3):
        for e in range(3):
            w = [win[(a * 3 + b) * 3 + e].astype(F32) for b in range(3)]
            blocks = (
                ((w[0], w[1]), (w[2], zero)),
                ((zero, w[0]), (w[1], w[2])),
            )
            for j in range(2):
                for q in range(2):
                    toep[pl.ds(e * 128 + j * 64, 64), pl.ds(a * 256 + q * 128, 128)] = jnp.concatenate(
                        blocks[j][q], axis=1
                    ).astype(BF16)

    lane = lax.broadcasted_iota(jnp.int32, (C, 128), 1)
    row = lax.broadcasted_iota(jnp.int32, (C, 128), 0)
    eye2 = (lax.rem(lane, C) == row).astype(F32)

    def conv(pair, p):
        pieces = []
        for a in range(3):
            for i in range(4):
                pieces.append(
                    jnp.concatenate([cells[x + a, 2 * p + i] for x in PAIRS[pair]], axis=1)
                )
        d = nn(toep[...], jnp.concatenate(pieces, axis=0))
        parts = []
        for h in range(2):
            for j in range(2):
                t = [
                    d[e * 128 + j * 64 : e * 128 + j * 64 + 64, h * 128 : h * 128 + 128] for e in range(3)
                ]
                before = jnp.where(lane == 0, 0.0, pltpu.roll(t[0], 1, 1))
                after = jnp.where(lane == NZ - 1, 0.0, pltpu.roll(t[2], NZ - 1, 1))
                parts.append(before + t[1] + after)
        return parts

    def keep(pair, p, parts):
        c = centre[...]
        parts = [v - c for v in parts]
        sums[...] += (parts[0] + parts[1]) + (parts[2] + parts[3])
        hi, lo = split(jnp.concatenate(parts, axis=1))
        both = jnp.concatenate([hi, lo], axis=0)
        held[pair * 8 + p] = both
        gram[...] += lax.dot_general(both, both, (((1,), (1,)), ((), ())), preferred_element_type=F32)

    gram[...] = jnp.zeros_like(gram)
    sums[...] = jnp.zeros_like(sums)
    first = conv(0, 1)
    total = (first[0] + first[1]) + (first[2] + first[3])
    mean0 = jnp.sum(total, axis=1, keepdims=True) * (1.0 / 512)
    centre[...] = jnp.broadcast_to(mean0, (C, 128))
    keep(0, 1, first)

    def one(pair, p):
        keep(pair, p, conv(pair, p))

    def several(pair, lo, hi):
        for p in range(lo, hi):
            one(pair, p)

    several(0, 2, 4)
    hear(0)
    tell(1)
    several(0, 4, 6)
    hear(1)
    tell(2)
    several(0, 6, 7)

    def clear(cond, x, y, nx, ny):
        @pl.when(cond)
        def _():
            cells[pl.ds(x, nx), pl.ds(y, ny)] = jnp.zeros((nx, ny, C, NZ), BF16)

    x_first, x_last = sx == 0, sx == n_x - 1
    y_first, y_last = sy == 0, sy == n_y - 1
    def arrive(q):
        start, size = PIECES[q]
        xcopies[2 * q].wait_recv()
        clear(x_last, BX + 1, start, 1, size)
        xcopies[2 * q + 1].wait_recv()
        clear(x_first, 0, start, 1, size)

    arrive(0)
    arrive(1)
    ccopies = []
    for d, x in enumerate((BX + 1, 0)):
        for f, (src_y, dst_y) in enumerate(((1, BY + 1), (BY, 0))):
            ccopies.append(
                send(
                    cells.at[x, src_y],
                    cells.at[x, dst_y],
                    cs_send.at[2 * d + f],
                    cs_recv.at[2 * d + f],
                    {"sy": at(n_y, sy, 2 * f - 1)},
                )
            )


    ycopies[0].wait_recv()
    clear(y_last, 1, BY + 1, BX, 1)
    ycopies[1].wait_recv()
    clear(y_first, 1, 0, BX, 1)
    several(0, 0, 1)
    several(0, 7, 8)

    def corner(f, y, y_edge):
        for d, (x, x_edge) in enumerate(((BX + 1, x_last), (0, x_first))):
            ccopies[2 * d + f].wait_recv()
            clear(jnp.logical_or(x_edge, y_edge), x, y, 1, 1)

    hear(2)
    for q in range(2, len(PIECES)):
        arrive(q)
        for p in READY[q]:
            if p == 0:
                corner(1, 0, y_first)
            elif p == 7:
                corner(0, BY + 1, y_last)
            one(1, p)

    def turned(col):
        return jnp.sum(eye2 * col, axis=0, keepdims=True)

    H = C // 2
    lane32, row32 = lane[:H], row[:H]
    low = lax.rem(lane32, C)

    def pack(v):
        top = v[:H]
        last = pltpu.roll(v[H:], 128 - H, 1)
        mixed = jnp.where(jnp.logical_and(low < H, row32 > low), last, top)
        diag = jnp.sum(jnp.where(low == row32, last, 0.0), axis=0, keepdims=True)
        return jnp.where(lane32[:16] < C, mixed[:16], mixed[16:]), diag

    dcol = jnp.sum(sums[...], axis=1, keepdims=True) * (1.0 / LOCAL)
    drow = turned(dcol)
    crow = turned(centre[:, 0:1])
    g = gram[:C] + gram[C:]
    g = g + pltpu.roll(g, C, 1)
    products, diag = pack(g - LOCAL * (dcol * drow))
    mean = crow + drow
    lane1 = lane[:1]

    def merge(products, diag, mean, count, n, me, others, moved, s_sem, r_sem):
        high = 8 if n <= 8 else 16
        rows = row[:high]
        line = jnp.where(lane1 < C, mean, jnp.where(lane1 < C + H, diag, 0.0))
        moved[me, pl.ds(0, 16)] = products
        moved[me, pl.ds(16, 1)] = line
        used = moved.at[me, pl.ds(0, 17)]
        copies = [
            send(used, used, s_sem.at[k], r_sem.at[k], device)
            for k, device in enumerate(others)
        ]
        for cp in copies:
            cp.wait_recv()
        def tree(parts):
            while len(parts) > 1:
                parts = [u + v for u, v in zip(parts[::2], parts[1::2])]
            return parts[0]

        total = tree([moved[i, pl.ds(0, 16)] for i in range(n)])
        means = tree([jnp.where(rows == i, moved[i, pl.ds(16, 1)], 0.0) for i in range(n)])
        line = jnp.sum(means, axis=0, keepdims=True)
        mean = jnp.where(lane1 < C, line * (1.0 / n), 0.0)
        off = jnp.where(jnp.logical_and(rows < n, lane[:high] < C), means - mean, 0.0)
        off = off + pltpu.roll(off, C, 1)
        oh, ol = (v.astype(F32) for v in split(off))
        rest = [jnp.zeros((8, 128), F32)] * (high == 8)
        outer = lax.dot_general(
            jnp.concatenate([oh, oh, ol] + rest, axis=0).astype(BF16),
            jnp.concatenate([oh, ol, oh] + rest, axis=0).astype(BF16),
            (((0,), (0,)), ((), ())),
            preferred_element_type=F32,
        )
        more, more_diag = pack(outer[:C])
        return total + count * more, line + count * more_diag, mean + pltpu.roll(mean, C, 1)

    count = float(LOCAL)
    state = merge(products, diag, mean, count, 2, core, [sibling], moved_c, rc_send, rc_recv)
    count *= 2
    state = merge(*state, count, n_x, sx, others_x, moved_x, rx_send, rx_recv)
    count *= n_x
    products, diag, mean = merge(
        *state, count, n_chip * n_b, chip * n_b + sb, others_p, moved_p, rp_send, rp_recv
    )

    half = jnp.concatenate([products, pltpu.roll(products, C, 1)], axis=0)
    across = jnp.concatenate([half, jnp.zeros((128 - H, 128), F32)], axis=0).T
    upper = jnp.where(jnp.logical_and(lane32 < H, row32 > lane32), across[:H], half)
    last = pltpu.roll(jnp.where(row32 > lane32, half, across[:H]), H, 1)
    last = jnp.where(lane32 == row32 + H, pltpu.roll(diag, 128 - H, 1), last)
    lower = jnp.where(lane32 < H, across[H:C], last)
    full = jnp.concatenate([upper, lower], axis=0)[:, :C]
    eye = eye2[:, :C]
    sigma = full * (1.0 / (LOCAL * n_x * n_y * n_b)) + 1e-05 * eye
    trace = jnp.sum(jnp.sum(sigma * eye, axis=1, keepdims=True), axis=0, keepdims=True)
    t = sigma / trace
    f = None
    for turn in range(NS_ITERS):
        step = 1.5 * eye - 0.5 * t
        f = step if f is None else mm(f, step)
        if turn < NS_ITERS - 1:
            t = mm(mm(t, step), step)
    gcp.wait()
    hcp.wait()
    v = vec[...]
    gain_col = jnp.sum(eye * v[0:1], axis=1, keepdims=True)
    shift_col = jnp.sum(eye * v[1:2], axis=1, keepdims=True)
    whiten = f / jnp.sqrt(trace) * gain_col
    bias = shift_col - jnp.sum(whiten * (mean - crow)[:, :C], axis=1, keepdims=True)
    offset[...] = jnp.broadcast_to(bias, (C, 128))
    wh, wl = split(whiten)
    mixer[...] = jnp.concatenate([wh.astype(F32), wh.astype(F32), wl.astype(F32)], axis=1).astype(BF16)
    for cp in sends:
        cp.wait_send()


def mix_body(held, mixer, offset, out, staged, sem):
    bias = offset[...]
    for pair in range(2):
        for p in range(8):
            both = held[pair * 8 + p]
            got = nn(mixer[...], jnp.concatenate([both, both[:C]], axis=0))
            for h in range(2):
                for j in range(2):
                    k = 2 * h + j
                    place = PAIRS[pair][h] * BY + 2 * p + j
                    staged[place] = got[:, k * 128 : k * 128 + 128] + bias
                    pltpu.make_async_copy(staged.at[place], out.at[:, place], sem).start()
    pltpu.make_async_copy(staged, out, sem).wait()


def on_device(volume, conv_weight, out_gain, out_shift):
    n_x, n_y, n_b = (lax.axis_size(a) for a in ("sx", "sy", "batch"))
    weight = jnp.transpose(conv_weight, (2, 3, 4, 0, 1)).reshape(27, C, C)
    anywhere = pl.BlockSpec(memory_space=pl.ANY)
    inside = pl.BlockSpec(memory_space=pltpu.VMEM)
    dma = pltpu.SemaphoreType.DMA
    n_p = n_y // 2 * n_b
    operands = (volume, weight, out_gain.reshape(1, C), out_shift.reshape(1, C))
    held, mixer, offset = pl.pallas_call(
        lambda *refs: body((n_x, n_y, n_b), *refs),
        out_shape=[
            jax.ShapeDtypeStruct((16, 2 * C, 512), BF16),
            jax.ShapeDtypeStruct((C, 3 * C), BF16),
            jax.ShapeDtypeStruct((C, 128), F32),
        ],
        in_specs=[anywhere] * 4,
        out_specs=[inside] * 3,
        scratch_shapes=[
            pltpu.VMEM((BX, C, BY, NZ), BF16),
            pltpu.VMEM((C * BY, NZ), F32),
            pltpu.VMEM((BX + 2, BY + 2, C, NZ), BF16),
            pltpu.VMEM((27, C, C), BF16),
            pltpu.VMEM((384, 768), BF16),
            pltpu.VMEM((2 * C, 2 * C), F32),
            pltpu.VMEM((C, 128), F32),
            pltpu.VMEM((C, 128), F32),
            pltpu.VMEM((2, 24, 128), F32),
            pltpu.VMEM((n_p, 24, 128), F32),
            pltpu.VMEM((n_x, 24, 128), F32),
            pltpu.VMEM((2, C), F32),
            dma((4,)),
            dma,
            dma((2,)),
            dma((2 * len(PIECES),)),
            dma((2 * len(PIECES),)),
            dma((2,)),
            dma((2,)),
            dma((4,)),
            dma((4,)),
            dma((1,)),
            dma((1,)),
            dma((n_p - 1,)),
            dma((n_p - 1,)),
            dma((n_x - 1,)),
            dma((n_x - 1,)),
            pltpu.SemaphoreType.REGULAR((3, 2)),
        ],
        compiler_params=pltpu.CompilerParams(
            collective_id=0, has_side_effects=True, vmem_limit_bytes=40 * 1024 * 1024
        ),
    )(*(pltpu.with_memory_space_constraint(v, pltpu.HBM) for v in operands))
    result = pl.pallas_call(
        mix_body,
        out_shape=jax.ShapeDtypeStruct((C, BX * BY, NZ), F32),
        in_specs=[inside] * 3,
        out_specs=anywhere,
        scratch_shapes=[pltpu.VMEM((BX * BY, C, NZ), F32), dma],
        compiler_params=pltpu.CompilerParams(vmem_limit_bytes=40 * 1024 * 1024),
    )(held, mixer, offset)
    return result.reshape(1, C, BX, BY, NZ)


def solution(mesh):
    in_specs = (P("batch", None, "sx", "sy", None), P(), P(), P())
    out_specs = P("batch", None, "sx", "sy", None)
    return jax.shard_map(
        on_device, mesh=mesh, in_specs=in_specs, out_specs=out_specs, check_vma=False
    )
```
